256 devices in a mesh: tm: 32 (over z_lo, y, core), space: 8 (over x, z_hi).
Axes of the slice: x: 4, y: 4, z: 8 (z_hi: 2, z_lo: 4; z = z_hi * 4 + z_lo), core: 2. Of those that a mesh axis runs over, the one named last changes fastest.
Arguments:
- video_q: bfloat16 [32768, 2048], P(('tm', 'space')), may hold values from -8 to 8
- video_k: bfloat16 [32768, 2048], P(('tm', 'space')), may hold values from -8 to 8
- video_v: bfloat16 [32768, 2048], P(('tm', 'space')), may hold values from -6 to 6
- video_grad: bfloat16 [32768, 2048], P(('tm', 'space')), may hold values from -6 to 6
- audio_q: bfloat16 [16384, 2048], P('tm', 'space'), may hold values from -8 to 8
- audio_k: bfloat16 [16384, 2048], P('tm', 'space'), may hold values from -8 to 8
- audio_v: bfloat16 [16384, 2048], P('tm', 'space'), may hold values from -6 to 6
- audio_grad: bfloat16 [16384, 2048], P('tm', 'space'), may hold values from -6 to 6
- intersection_blocks: int32 [32, 2], replicated, may hold values from 0 to 1, as said below
- intersection_rows: int32 [32, 2], replicated, may hold values from 0 to 256, as said below
Outputs:
- video_out: bfloat16 [32768, 2048], P(('tm', 'space'))
- d_video_q: bfloat16 [32768, 2048], P(('tm', 'space'))
- d_video_k: bfloat16 [32768, 2048], P(('tm', 'space'))
- d_video_v: bfloat16 [32768, 2048], P(('tm', 'space'))
- audio_out: bfloat16 [16384, 2048], P('tm', 'space')
- d_audio_q: bfloat16 [16384, 2048], P('tm', 'space')
- d_audio_k: bfloat16 [16384, 2048], P('tm', 'space')
- d_audio_v: bfloat16 [16384, 2048], P('tm', 'space')
The draws below stay inside these ranges and needn't reach their ends.
Inputs may be any that keep to these rules, and one draw needn't show every extreme that they name: `intersection_blocks`: entry [t, 0] counts an audio block of time block t - 1 and entry [t, 1] one of time block t + 1, from 0 within that time block. `intersection_rows`: entry [t, j] is 0 where that neighbouring time block does not exist (j = 0 in the first time block, j = 1 in the last).
All inputs are finite; a program needn't handle non-finite values.
Results may differ from the reference program's by a relative error of at most 0.0096.
Values may be sent and summed in bfloat16 or wider, within the bound.
A program may use at most 128 MiB of HBM per device.

```python
import jax
import jax.numpy as jnp
from jax import lax

D = 2048
HEADS = 16
HEAD_DIM = 128
AB = 2
BLOCK = 256
POOL = 16
VB = 1024
A_TM = 512
PV = 64
VT = 32768
AT = 16384
N_TM = 32


def draw_video_q(key, part):
    key = jax.random.fold_in(key, 1)
    sample = jnp.clip(1.5 * jax.random.normal(key, (VT, D), jnp.float32), -8.0, 8.0)
    return sample.astype(jnp.bfloat16)


def draw_video_k(key, part):
    key = jax.random.fold_in(key, 2)
    sample = jnp.clip(1.5 * jax.random.normal(key, (VT, D), jnp.float32), -8.0, 8.0)
    return sample.astype(jnp.bfloat16)


def draw_audio_q(key, part):
    key = jax.random.fold_in(key, 3)
    sample = jnp.clip(1.5 * jax.random.normal(key, (AT, D), jnp.float32), -8.0, 8.0)
    return sample.astype(jnp.bfloat16)


def draw_audio_k(key, part):
    key = jax.random.fold_in(key, 4)
    sample = jnp.clip(1.5 * jax.random.normal(key, (AT, D), jnp.float32), -8.0, 8.0)
    return sample.astype(jnp.bfloat16)


def draw_intersection_blocks(key, part):
    key = jax.random.fold_in(key, 5)
    return jax.random.randint(key, (N_TM, 2), 0, AB, dtype=jnp.int32)


def draw_intersection_rows(key, part):
    key = jax.random.fold_in(key, 6)
    counts = jax.random.randint(jax.random.fold_in(key, 1), (N_TM, 2), 1, BLOCK + 1, dtype=jnp.int32)
    chosen = jax.random.randint(jax.random.fold_in(key, 2), (), 1, N_TM - 1, dtype=jnp.int32)
    stamps = jnp.arange(N_TM, dtype=jnp.int32)[:, None]
    slots = jnp.arange(2, dtype=jnp.int32)[None, :]
    counts = jnp.where(stamps == chosen, BLOCK, counts)
    counts = jnp.where((stamps == 0) & (slots == 0), 0, counts)
    counts = jnp.where((stamps == N_TM - 1) & (slots == 1), 0, counts)
    return counts.astype(jnp.int32)


def steps_of(stream_key, shape, split, least, largest):
    gain = 1.0
    for position, blocks in split:
        heights = jax.random.uniform(jax.random.fold_in(jax.random.fold_in(stream_key, 6), position), (blocks,), jnp.float32, least / len(split), largest / len(split))
        gain = gain * jnp.repeat(jnp.exp(heights), shape[position] // blocks).reshape((-1,) + (1,) * (len(shape) - 1 - position))
    return gain


def normal_values(key, shape, scale, reach, shards=(), kind=jnp.bfloat16):
    entries = scale * jax.random.normal(key, shape, jnp.float32)
    if shards:
        entries = entries * steps_of(key, shape, shards, -0.22, 0.18)
    return jnp.clip(entries, -reach, reach).astype(kind)


def setup_inputs(seed: int = 0) -> dict:
    splits = jax.random.split(jax.random.key(seed), 11)
    return {
        "video_q": draw_video_q(jax.random.fold_in(splits[10], 71), 0),
        "video_k": draw_video_k(jax.random.fold_in(splits[10], 71), 0),
        "video_v": normal_values(splits[2], (VT, D), 1.0, 6.0, ((0, 256),)),
        "video_grad": normal_values(splits[3], (VT, D), 1.0, 6.0, ((0, 256),)),
        "audio_q": draw_audio_q(jax.random.fold_in(splits[10], 71), 0),
        "audio_k": draw_audio_k(jax.random.fold_in(splits[10], 71), 0),
        "audio_v": normal_values(splits[6], (AT, D), 1.0, 6.0, ((0, 32), (1, 8))),
        "audio_grad": normal_values(splits[7], (AT, D), 1.0, 6.0, ((0, 32), (1, 8))),
        "intersection_blocks": draw_intersection_blocks(jax.random.fold_in(splits[10], 71), 0),
        "intersection_rows": draw_intersection_rows(jax.random.fold_in(splits[10], 71), 0),
    }


def attend(queries, key_list, value_list, grad_out, allowed):
    factor = queries.shape[-1] ** -0.5
    query_wide = queries.astype(jnp.float32)
    key_wide = key_list.astype(jnp.float32)
    value_wide = value_list.astype(jnp.float32)
    grad_wide = grad_out.astype(jnp.float32)
    highest = lax.Precision.HIGHEST
    scores = jnp.einsum("qhd,khd->hqk", query_wide, key_wide, precision=highest) * factor
    masked = jnp.where(allowed[None, None, :], scores, -jnp.inf)
    row_max = jnp.max(masked, axis=2, keepdims=True)
    raised = jnp.exp(masked - row_max)
    shares = lax.optimization_barrier((raised / jnp.sum(raised, axis=2, keepdims=True)).astype(jnp.bfloat16))
    shares_wide = shares.astype(jnp.float32)
    output_wide = jnp.einsum("hqk,khd->qhd", shares_wide, value_wide, precision=highest)
    output = output_wide.astype(jnp.bfloat16)
    grad_values = jnp.einsum("hqk,qhd->khd", shares_wide, grad_wide, precision=highest)
    grad_shares = jnp.einsum("qhd,khd->hqk", grad_wide, value_wide, precision=highest)
    correction = jnp.transpose(jnp.sum(grad_wide * output_wide, axis=2))[:, :, None]
    grad_scores = lax.optimization_barrier((shares_wide * (grad_shares - correction) * factor).astype(jnp.bfloat16))
    scores_wide = grad_scores.astype(jnp.float32)
    grad_query = jnp.einsum("hqk,khd->qhd", scores_wide, key_wide, precision=highest)
    grad_keys = jnp.einsum("hqk,qhd->khd", scores_wide, query_wide, precision=highest)
    return output, grad_query, grad_keys, grad_values


def reference(video_q, video_k, video_v, video_grad, audio_q, audio_k, audio_v, audio_grad, intersection_blocks, intersection_rows):
    video_queries = video_q.reshape(N_TM, VB, HEADS, HEAD_DIM)
    video_keys = video_k.reshape(N_TM, VB, HEADS, HEAD_DIM)
    video_values = video_v.reshape(N_TM, VB, HEADS, HEAD_DIM)
    video_grads = video_grad.reshape(N_TM, VB, HEADS, HEAD_DIM)
    audio_queries = audio_q.reshape(N_TM, A_TM, HEADS, HEAD_DIM)
    audio_keys = audio_k.reshape(N_TM, A_TM, HEADS, HEAD_DIM)
    audio_values = audio_v.reshape(N_TM, A_TM, HEADS, HEAD_DIM)
    audio_grads = audio_grad.reshape(N_TM, A_TM, HEADS, HEAD_DIM)
    flat_keys = audio_k.reshape(N_TM * A_TM, HEADS, HEAD_DIM)
    flat_values = audio_v.reshape(N_TM * A_TM, HEADS, HEAD_DIM)
    pool_factor = POOL ** -0.5

    def pool_pairs(source):
        grouped = source.reshape(N_TM, PV, POOL, HEADS, HEAD_DIM).astype(jnp.float32)
        return (jnp.sum(grouped, axis=2) * pool_factor).astype(jnp.bfloat16)

    padding = jnp.zeros((1, PV, HEADS, HEAD_DIM), jnp.bfloat16)
    padded_keys = jnp.concatenate([padding, pool_pairs(video_k), padding], axis=0)
    padded_values = jnp.concatenate([padding, pool_pairs(video_v), padding], axis=0)
    stamps = jnp.arange(N_TM, dtype=jnp.int32)
    last_start = N_TM * A_TM - BLOCK
    earlier_start = jnp.clip(((stamps - 1) * AB + intersection_blocks[:, 0]) * BLOCK, 0, last_start).astype(jnp.int32)
    later_start = jnp.clip(((stamps + 1) * AB + intersection_blocks[:, 1]) * BLOCK, 0, last_start).astype(jnp.int32)
    positions = jnp.arange(BLOCK, dtype=jnp.int32)

    def video_part(moment):
        key_list = jnp.concatenate([video_keys[moment], audio_keys[moment],
                                    lax.dynamic_slice_in_dim(flat_keys, earlier_start[moment], BLOCK, 0),
                                    lax.dynamic_slice_in_dim(flat_keys, later_start[moment], BLOCK, 0)], axis=0)
        value_list = jnp.concatenate([video_values[moment], audio_values[moment],
                                      lax.dynamic_slice_in_dim(flat_values, earlier_start[moment], BLOCK, 0),
                                      lax.dynamic_slice_in_dim(flat_values, later_start[moment], BLOCK, 0)], axis=0)
        allowed = jnp.concatenate([jnp.ones((VB + A_TM,), bool), positions < intersection_rows[moment, 0],
                                   positions < intersection_rows[moment, 1]])
        return attend(video_queries[moment], key_list, value_list, video_grads[moment], allowed)

    def audio_part(moment):
        key_list = jnp.concatenate([audio_keys[moment],
                                    lax.dynamic_slice_in_dim(padded_keys, moment, 3, 0).reshape(3 * PV, HEADS, HEAD_DIM)], axis=0)
        value_list = jnp.concatenate([audio_values[moment],
                                      lax.dynamic_slice_in_dim(padded_values, moment, 3, 0).reshape(3 * PV, HEADS, HEAD_DIM)], axis=0)
        allowed = jnp.concatenate([jnp.ones((A_TM,), bool), jnp.full((PV,), moment > 0), jnp.ones((PV,), bool),
                                   jnp.full((PV,), moment < N_TM - 1)])
        return attend(audio_queries[moment], key_list, value_list, audio_grads[moment], allowed)

    video_result = lax.map(video_part, stamps)
    audio_result = lax.map(audio_part, stamps)
    rim_start = VB + A_TM

    def audio_total(video_terms, audio_terms):
        flat_grads = (video_terms[:, VB:rim_start] + audio_terms[:, :A_TM]).reshape(N_TM * A_TM, HEADS, HEAD_DIM)
        flat_grads = flat_grads.at[earlier_start[:, None] + positions[None, :]].add(video_terms[:, rim_start:rim_start + BLOCK])
        flat_grads = flat_grads.at[later_start[:, None] + positions[None, :]].add(video_terms[:, rim_start + BLOCK:])
        return flat_grads.reshape(N_TM * A_TM, D).astype(jnp.bfloat16)

    def video_total(video_terms, audio_terms):
        pooled_terms = audio_terms[:, A_TM:].reshape(N_TM, 3, PV, HEADS, HEAD_DIM)
        summed = jnp.zeros((N_TM + 2, PV, HEADS, HEAD_DIM), jnp.float32)
        for offset in range(3):
            summed = summed.at[offset:offset + N_TM].add(pooled_terms[:, offset])
        summed = summed[1:N_TM + 1]
        spread = video_terms[:, :VB].reshape(N_TM, PV, POOL, HEADS, HEAD_DIM) + summed[:, :, None] * pool_factor
        return spread.reshape(N_TM * VB, D).astype(jnp.bfloat16)

    return (video_result[0].reshape(N_TM * VB, D),
            video_result[1].reshape(N_TM * VB, D).astype(jnp.bfloat16),
            video_total(video_result[2], audio_result[2]),
            video_total(video_result[3], audio_result[3]),
            audio_result[0].reshape(N_TM * A_TM, D),
            audio_result[1].reshape(N_TM * A_TM, D).astype(jnp.bfloat16),
            audio_total(video_result[2], audio_result[2]),
            audio_total(video_result[3], audio_result[3]))
```

```python
import jax
import jax.numpy as jnp
from jax import lax
from jax.experimental import pallas as pl
from jax.experimental.pallas import tpu as pltpu
from jax.sharding import PartitionSpec as P

HEAD = 128
CHUNK = 256
POOL = 16
HEADS_HERE = 2
VIDEO = 1024
AUDIO = 512
POOLED = 64
OWN = VIDEO
BEFORE = VIDEO + AUDIO
AFTER = BEFORE + CHUNK
SHARED = AFTER + CHUNK
LISTED = SHARED + CHUNK
FACTOR = HEAD**-0.5
LOG2E = 1.4426950408889634
MESH = pl.DeviceIdType.MESH
F32 = jnp.float32
BF16 = jnp.bfloat16


def dot(a, b, contract=((1,), (0,))):
    return lax.dot_general(a, b, (contract, ((), ())), preferred_element_type=F32)


def kernel(
    video_q,
    video_k,
    video_v,
    video_g,
    audio_q,
    audio_k,
    audio_v,
    audio_g,
    blocks,
    rows,
    out_vo,
    out_vdq,
    out_vdk,
    out_vdv,
    out_ao,
    out_adq,
    out_adk,
    out_adv,
    keys,
    values,
    queries,
    grads,
    sound_q,
    sound_g,
    keys_t,
    values_t,
    key_sum,
    value_sum,
    scores,
    shares,
    pool_map,
    video_out,
    audio_out,
    rim_out,
    rim_grad_out,
    rim_grad_in,
    pool_grad_out,
    pool_grad_in,
    sound_sum,
    in_send,
    in_recv,
    out_send,
    out_recv,
    near_send,
    near_recv,
    local_in,
    local_sound,
    local_out,
    local_sound_out,
):
    tm = lax.axis_index("tm")
    me = lax.axis_index("space")
    x, half = lax.div(me, 2), lax.rem(me, 2)
    has_prev, has_next = tm > 0, tm < lax.axis_size("tm") - 1
    sides = ((has_prev, tm - 1), (has_next, tm + 1))

    def target(r):
        return lax.rem(x + lax.div(r, 2), 4) * 2 + lax.rem(half + lax.rem(r, 2), 2)

    def origin(r):
        return lax.rem(x + 4 - lax.div(r, 2), 4) * 2 + lax.rem(half + lax.rem(r, 2), 2)

    def rows_of(s):
        return pl.ds(pl.multiple_of(s * HEAD, HEAD), HEAD)

    def columns_of(s, j):
        return pl.ds(pl.multiple_of((s * HEADS_HERE + j) * HEAD, HEAD), HEAD)

    def head_columns(j):
        return pl.ds(pl.multiple_of(j * HEAD, HEAD), HEAD)

    sources = (video_k, video_v, video_q, video_g)
    landings = (keys, values, queries, grads)
    results = (out_vo, out_vdq, out_vdk, out_vdv)

    def in_copy(j, a, r, sender):
        s = target(r)
        slot = rows_of(me if sender else origin(r))
        index = (j * 4 + a) * 8 + r
        return pltpu.make_async_remote_copy(
            src_ref=sources[a].at[:, columns_of(s, j)],
            dst_ref=landings[a].at[j, slot, :],
            send_sem=in_send.at[index],
            recv_sem=in_recv.at[index],
            device_id=(tm, s),
            device_id_type=MESH,
        )

    def in_local(j, a):
        return pltpu.make_async_copy(
            sources[a].at[:, columns_of(me, j)],
            landings[a].at[j, rows_of(me), :],
            local_in.at[j * 4 + a],
        )

    def out_copy(j, a, r, sender):
        s = target(r)
        slot = columns_of(me if sender else origin(r), j)
        index = (j * 4 + a) * 8 + r
        return pltpu.make_async_remote_copy(
            src_ref=video_out.at[a, j, rows_of(s), :],
            dst_ref=results[a].at[:, slot],
            send_sem=out_send.at[index],
            recv_sem=out_recv.at[index],
            device_id=(tm, s),
            device_id_type=MESH,
        )

    def out_local(j, a):
        return pltpu.make_async_copy(
            video_out.at[a, j, rows_of(me), :],
            results[a].at[:, columns_of(me, j)],
            local_out.at[j * 4 + a],
        )

    sound_sources = (audio_k, audio_v, audio_q, audio_g)

    def sound_local(j, a):
        landing = (
            keys.at[j, pl.ds(OWN, AUDIO), :],
            values.at[j, pl.ds(OWN, AUDIO), :],
            sound_q.at[j],
            sound_g.at[j],
        )[a]
        return pltpu.make_async_copy(
            sound_sources[a].at[:, head_columns(j)], landing, local_sound.at[j * 4 + a]
        )

    sound_results = (out_ao, out_adq, out_adk, out_adv)

    def sound_out(j, a):
        return pltpu.make_async_copy(
            audio_out.at[a, j],
            sound_results[a].at[:, head_columns(j)],
            local_sound_out.at[j * 4 + a],
        )

    def near_copy(src, dst, index, device):
        return pltpu.make_async_remote_copy(
            src_ref=src,
            dst_ref=dst,
            send_sem=near_send.at[index],
            recv_sem=near_recv.at[index],
            device_id=(device, me),
            device_id_type=MESH,
        )

    def rim_copy(j, a, d):
        return near_copy(
            rim_out.at[d, a, j],
            (keys, values)[a].at[j, pl.ds((AFTER, BEFORE)[d], CHUNK), :],
            (j * 2 + a) * 2 + d,
            sides[d][1],
        )

    def pooled_copy(j, a, d):
        listed = (keys, values)[a]
        return near_copy(
            listed.at[j, pl.ds(SHARED + POOLED, POOLED), :],
            listed.at[j, pl.ds(SHARED + (2 * POOLED, 0)[d], POOLED), :],
            8 + (j * 2 + a) * 2 + d,
            sides[d][1],
        )

    def pool_grad_copy(j, d):
        return near_copy(
            pool_grad_out.at[d, j], pool_grad_in.at[d, j], 16 + j * 2 + d, sides[d][1]
        )

    def rim_grad_copy(j, d):
        return near_copy(
            rim_grad_out.at[d, j], rim_grad_in.at[d, j], 20 + j * 2 + d, sides[d][1]
        )

    def on_sides(act):
        for d in range(2):

            @pl.when(sides[d][0])
            def _():
                act(d)

    def from_sides(act):
        for d in range(2):

            @pl.when(sides[1 - d][0])
            def _():
                act(d)

    barrier = pltpu.get_barrier_semaphore()

    def greet(r, carry):
        pl.semaphore_signal(barrier, inc=1, device_id=(tm, target(r)), device_id_type=MESH)
        return carry

    lax.fori_loop(1, 8, greet, 0)
    on_sides(
        lambda d: pl.semaphore_signal(
            barrier, inc=1, device_id=(sides[d][1], me), device_id_type=MESH
        )
    )
    for j in range(HEADS_HERE):
        for a in range(4):
            sound_local(j, a).start()
    for j in range(HEADS_HERE):
        for a in range(4):
            in_local(j, a).start()
    pl.semaphore_wait(barrier, 7 + has_prev.astype(jnp.int32) + has_next.astype(jnp.int32))

    def send_head(j):
        for a in range(4):

            def across(i, carry, a=a):
                in_copy(j, a, 2 * i + 1, True).start()
                return carry

            def along(i, carry, a=a):
                in_copy(j, a, 2 * i, True).start()
                return carry

            lax.fori_loop(0, 4, across, 0)
            lax.fori_loop(1, 4, along, 0)

    send_head(0)

    for j in range(HEADS_HERE):
        for a in range(2):
            sound_local(j, a).wait()

    def stage_rims(d):
        weight = blocks[sides[d][1], 1 - d].astype(F32)
        for j in range(HEADS_HERE):
            for a in range(2):
                listed = (keys, values)[a]
                first = listed[j, OWN : OWN + CHUNK, :].astype(F32)
                second = listed[j, OWN + CHUNK : BEFORE, :].astype(F32)
                rim_out[d, a, j] = (first * (1.0 - weight) + second * weight).astype(BF16)
                rim_copy(j, a, d).start()

    on_sides(stage_rims)

    def fill_rims(d):
        spare = jnp.zeros((HEADS_HERE, CHUNK, HEAD), BF16)
        gone = jnp.zeros((HEADS_HERE, POOLED, HEAD), BF16)
        rim_at, pool_at = (AFTER, BEFORE)[d], SHARED + (2 * POOLED, 0)[d]
        for listed in (keys, values):
            listed[:, rim_at : rim_at + CHUNK, :] = spare
            listed[:, pool_at : pool_at + POOLED, :] = gone
        rim_grad_in[d] = jnp.zeros((HEADS_HERE, 2, CHUNK, HEAD), BF16)
        pool_grad_in[d] = jnp.zeros((HEADS_HERE, 2, POOLED, HEAD), BF16)

    for d in range(2):

        @pl.when(jnp.logical_not(sides[1 - d][0]))
        def _():
            fill_rims(d)

    for listed in (keys, values):
        listed[:, SHARED + 3 * POOLED :, :] = jnp.zeros((HEADS_HERE, POOLED, HEAD), BF16)
    group = lax.shift_right_logical(lax.broadcasted_iota(jnp.int32, (POOLED, VIDEO), 1), 4)
    member = group == lax.broadcasted_iota(jnp.int32, (POOLED, VIDEO), 0)
    pool_map[...] = jnp.where(member, 1.0, 0.0).astype(BF16)

    for a in range(4):
        lax.fori_loop(1, 8, lambda r, c, a=a: (in_copy(0, a, r, True).wait_send(), c)[1], 0)
    send_head(1)

    live = (rows[tm, 0], rows[tm, 1])
    place = lax.broadcasted_iota(jnp.int32, (CHUNK, CHUNK), 0)
    first_pooled = jnp.where(has_prev, 0, POOLED)
    last_pooled = jnp.where(has_next, 3 * POOLED, 2 * POOLED)
    video_chunks = tuple(range(8))
    audio_chunks = (4, 5, 8)

    def mask(c, s):
        if c == 6:
            return jnp.where(place < live[0], s, -jnp.inf)
        if c == 7:
            return jnp.where(place < live[1], s, -jnp.inf)
        if c == 8:
            return jnp.where((place >= first_pooled) & (place < last_pooled), s, -jnp.inf)
        return s

    def span(c):
        return slice(c * CHUNK, (c + 1) * CHUNK)

    def attend(j, chunks, q, g):
        top = None
        for i, c in enumerate(chunks):
            s = mask(c, dot(keys[j, span(c), :], q, ((1,), (1,))))
            scores[span(i), :] = s
            peak = jnp.max(s, axis=0, keepdims=True)
            top = peak if top is None else jnp.maximum(top, peak)
        total = jnp.zeros((1, CHUNK), F32)
        for i, c in enumerate(chunks):
            e = jnp.exp2((scores[span(i), :] - top) * (FACTOR * LOG2E))
            scores[span(i), :] = e
            total = total + jnp.sum(e, axis=0, keepdims=True)
        inverse = 1.0 / total
        output = jnp.zeros((HEAD, CHUNK), F32)
        for i, c in enumerate(chunks):
            p = (scores[span(i), :] * inverse).astype(BF16)
            shares[span(i), :] = p
            output = output + dot(values_t[:, span(c)], p)
            value_sum[span(c), :] += dot(p, g)
        correction = jnp.sum(g.astype(F32).T * output, axis=0, keepdims=True)
        query_grad = jnp.zeros((HEAD, CHUNK), F32)
        for i, c in enumerate(chunks):
            dp = dot(values[j, span(c), :], g, ((1,), (1,)))
            ds = (shares[span(i), :].astype(F32) * (dp - correction) * FACTOR).astype(BF16)
            query_grad = query_grad + dot(keys_t[:, span(c)], ds)
            key_sum[span(c), :] += dot(ds, q)
        return output.T.astype(BF16), query_grad.T.astype(BF16)

    def head(j, carry):
        for a in range(2):
            in_local(j, a).wait()
            lax.fori_loop(1, 8, lambda r, c, a=a: (in_copy(j, a, r, False).wait_recv(), c)[1], 0)
        for a, listed in enumerate((keys, values)):
            pooled = dot(pool_map[...], listed[j, :VIDEO, :]) * (POOL**-0.5)
            listed[j, SHARED + POOLED : SHARED + 2 * POOLED, :] = pooled.astype(BF16)
            on_sides(lambda d, a=a: pooled_copy(j, a, d).start())
        for a in range(2):
            from_sides(lambda d, a=a: rim_copy(j, a, d).wait_recv())
        for c in range(8):
            keys_t[:, span(c)] = keys[j, span(c), :].astype(F32).T.astype(BF16)
            values_t[:, span(c)] = values[j, span(c), :].astype(F32).T.astype(BF16)
        key_sum[...] = jnp.zeros_like(key_sum)
        value_sum[...] = jnp.zeros_like(value_sum)
        for a in range(2):
            from_sides(lambda d, a=a: pooled_copy(j, a, d).wait_recv())
        keys_t[:, span(8)] = keys[j, span(8), :].astype(F32).T.astype(BF16)
        values_t[:, span(8)] = values[j, span(8), :].astype(F32).T.astype(BF16)
        for a in (2, 3):
            sound_local(j, a).wait()

        def sound_step(i, c):
            part = pl.ds(pl.multiple_of(i * CHUNK, CHUNK), CHUNK)
            o, dq = attend(j, audio_chunks, sound_q[j, part, :], sound_g[j, part, :])
            audio_out[0, j, part, :] = o
            audio_out[1, j, part, :] = dq
            return c

        lax.fori_loop(0, AUDIO // CHUNK, sound_step, 0)
        sound_out(j, 0).start()
        sound_out(j, 1).start()
        for d in range(2):
            at = SHARED + (0, 2 * POOLED)[d]
            pool_grad_out[d, j, 0] = key_sum[at : at + POOLED, :].astype(BF16)
            pool_grad_out[d, j, 1] = value_sum[at : at + POOLED, :].astype(BF16)
        on_sides(lambda d: pool_grad_copy(j, d).start())

        for a in (2, 3):
            in_local(j, a).wait()
            lax.fori_loop(1, 8, lambda r, c, a=a: (in_copy(j, a, r, False).wait_recv(), c)[1], 0)

        def video_step(k, c):
            i = lax.rem(x + k, 4)
            part = pl.ds(pl.multiple_of(i * CHUNK, CHUNK), CHUNK)
            o, dq = attend(j, video_chunks, queries[j, part, :], grads[j, part, :])
            video_out[0, j, part, :] = o
            video_out[1, j, part, :] = dq
            for a in range(2):
                out_copy(j, a, 2 * k + 1, True).start()

                @pl.when(k == 0)
                def _(a=a):
                    out_local(j, a).start()

                @pl.when(k > 0)
                def _(a=a):
                    out_copy(j, a, 2 * k, True).start()

            return c

        lax.fori_loop(0, 4, video_step, 0)
        for d in range(2):
            at = (BEFORE, AFTER)[d]
            rim_grad_out[d, j, 0] = key_sum[at : at + CHUNK, :].astype(BF16)
            rim_grad_out[d, j, 1] = value_sum[at : at + CHUNK, :].astype(BF16)
        on_sides(lambda d: rim_grad_copy(j, d).start())
        from_sides(lambda d: pool_grad_copy(j, d).wait_recv())
        for a, summed in enumerate((key_sum, value_sum)):
            pooled = summed[SHARED + POOLED : SHARED + 2 * POOLED, :]
            for d in range(2):
                pooled = pooled + pool_grad_in[d, j, a].astype(F32)
            pooled = pooled * (POOL**-0.5)
            spread = jnp.broadcast_to(pooled[:, None, :], (POOLED, POOL, HEAD))
            whole = summed[:VIDEO, :] + spread.reshape(VIDEO, HEAD)
            video_out[2 + a, j] = whole.astype(BF16)
            out_local(j, 2 + a).start()

            def across(i, c, a=a):
                out_copy(j, 2 + a, 2 * i + 1, True).start()
                return c

            def along(i, c, a=a):
                out_copy(j, 2 + a, 2 * i, True).start()
                return c

            lax.fori_loop(0, 4, across, 0)
            lax.fori_loop(1, 4, along, 0)
            sound_sum[j, a] = summed[OWN:BEFORE, :]
        return carry

    lax.fori_loop(0, HEADS_HERE, head, 0)

    prev_weight = blocks[jnp.maximum(tm - 1, 0), 1].astype(F32)
    next_weight = blocks[jnp.minimum(tm + 1, lax.axis_size("tm") - 1), 0].astype(F32)
    weights = (next_weight, prev_weight)
    for j in range(HEADS_HERE):
        from_sides(lambda d, j=j: rim_grad_copy(j, d).wait_recv())
        for a in range(2):
            for b in range(2):
                part = slice(b * CHUNK, (b + 1) * CHUNK)
                whole = sound_sum[j, a, part, :]
                for d in range(2):
                    weight = weights[d] if b else 1.0 - weights[d]
                    whole = whole + rim_grad_in[d, j, a].astype(F32) * weight
                audio_out[2 + a, j, part, :] = whole.astype(BF16)
            sound_out(j, 2 + a).start()

    for j in range(HEADS_HERE):
        for a in range(4):
            sound_out(j, a).wait()
            out_local(j, a).wait()
            lax.fori_loop(1, 8, lambda r, c, j=j, a=a: (out_copy(j, a, r, True).wait_send(), c)[1], 0)
            lax.fori_loop(1, 8, lambda r, c, j=j, a=a: (out_copy(j, a, r, False).wait_recv(), c)[1], 0)
        for a in range(2):
            on_sides(lambda d, j=j, a=a: rim_copy(j, a, d).wait_send())
            on_sides(lambda d, j=j, a=a: pooled_copy(j, a, d).wait_send())
        on_sides(lambda d, j=j: pool_grad_copy(j, d).wait_send())
        on_sides(lambda d, j=j: rim_grad_copy(j, d).wait_send())
    for a in range(4):
        lax.fori_loop(1, 8, lambda r, c, a=a: (in_copy(1, a, r, True).wait_send(), c)[1], 0)


def per_device(*args):
    video = jax.ShapeDtypeStruct(args[0].shape, BF16)
    audio = jax.ShapeDtypeStruct(args[4].shape, BF16)
    two = HEADS_HERE
    return pl.pallas_call(
        kernel,
        out_shape=(video,) * 4 + (audio,) * 4,
        in_specs=[pl.BlockSpec(memory_space=pl.ANY)] * 8
        + [pl.BlockSpec(memory_space=pltpu.SMEM)] * 2,
        out_specs=(pl.BlockSpec(memory_space=pl.ANY),) * 8,
        scratch_shapes=[
            pltpu.VMEM((two, LISTED, HEAD), BF16),
            pltpu.VMEM((two, LISTED, HEAD), BF16),
            pltpu.VMEM((two, VIDEO, HEAD), BF16),
            pltpu.VMEM((two, VIDEO, HEAD), BF16),
            pltpu.VMEM((two, AUDIO, HEAD), BF16),
            pltpu.VMEM((two, AUDIO, HEAD), BF16),
            pltpu.VMEM((HEAD, LISTED), BF16),
            pltpu.VMEM((HEAD, LISTED), BF16),
            pltpu.VMEM((LISTED, HEAD), F32),
            pltpu.VMEM((LISTED, HEAD), F32),
            pltpu.VMEM((SHARED, CHUNK), F32),
            pltpu.VMEM((SHARED, CHUNK), BF16),
            pltpu.VMEM((POOLED, VIDEO), BF16),
            pltpu.VMEM((4, two, VIDEO, HEAD), BF16),
            pltpu.VMEM((4, two, AUDIO, HEAD), BF16),
            pltpu.VMEM((2, 2, two, CHUNK, HEAD), BF16),
            pltpu.VMEM((2, two, 2, CHUNK, HEAD), BF16),
            pltpu.VMEM((2, two, 2, CHUNK, HEAD), BF16),
            pltpu.VMEM((2, two, 2, POOLED, HEAD), BF16),
            pltpu.VMEM((2, two, 2, POOLED, HEAD), BF16),
            pltpu.VMEM((two, 2, AUDIO, HEAD), F32),
            pltpu.SemaphoreType.DMA((64,)),
            pltpu.SemaphoreType.DMA((64,)),
            pltpu.SemaphoreType.DMA((64,)),
            pltpu.SemaphoreType.DMA((64,)),
            pltpu.SemaphoreType.DMA((24,)),
            pltpu.SemaphoreType.DMA((24,)),
            pltpu.SemaphoreType.DMA((8,)),
            pltpu.SemaphoreType.DMA((8,)),
            pltpu.SemaphoreType.DMA((8,)),
            pltpu.SemaphoreType.DMA((8,)),
        ],
        compiler_params=pltpu.CompilerParams(
            collective_id=0, has_side_effects=True, vmem_limit_bytes=48 * 1024 * 1024
        ),
        name="joint_attention",
    )(*args)


def solution(mesh):
    tokens, sound = P(("tm", "space"), None), P("tm", "space")
    return jax.shard_map(
        per_device,
        mesh=mesh,
        in_specs=(tokens,) * 4 + (sound,) * 4 + (P(), P()),
        out_specs=(tokens,) * 4 + (sound,) * 4,
        check_vma=False,
    )
```

```python
import jax
import jax.numpy as jnp
from jax import lax
from jax.experimental import pallas as pl
from jax.experimental.pallas import tpu as pltpu
from jax.sharding import PartitionSpec as P

HEAD = 128
CHUNK = 256
POOL = 16
HEADS_HERE = 2
VIDEO = 1024
AUDIO = 512
POOLED = 64
OWN = VIDEO
BEFORE = VIDEO + AUDIO
AFTER = BEFORE + CHUNK
SHARED = AFTER + CHUNK
LISTED = SHARED + CHUNK
FACTOR = HEAD**-0.5
LOG2E = 1.4426950408889634
MESH = pl.DeviceIdType.MESH
F32 = jnp.float32
BF16 = jnp.bfloat16


def dot(a, b, contract=((1,), (0,))):
    return lax.dot_general(a, b, (contract, ((), ())), preferred_element_type=F32)


def kernel(
    video_q,
    video_k,
    video_v,
    video_g,
    audio_q,
    audio_k,
    audio_v,
    audio_g,
    blocks,
    rows,
    out_vo,
    out_vdq,
    out_vdk,
    out_vdv,
    out_ao,
    out_adq,
    out_adk,
    out_adv,
    keys,
    values,
    queries,
    grads,
    sound_q,
    sound_g,
    keys_t,
    values_t,
    key_sum,
    value_sum,
    scores,
    shares,
    rows_k,
    rows_v,
    pool_stage,
    pool_land,
    video_out,
    audio_out,
    rim_out,
    rim_grad_out,
    rim_grad_in,
    pool_grad_out,
    pool_grad_in,
    in_send,
    in_recv,
    out_send,
    out_recv,
    near_send,
    near_recv,
    pool_send,
    pool_recv,
    local_rows,
    local_in,
    local_sound,
    local_out,
    local_sound_out,
):
    tm = lax.axis_index("tm")
    me = lax.axis_index("space")
    x, half = lax.div(me, 2), lax.rem(me, 2)
    has_prev, has_next = tm > 0, tm < lax.axis_size("tm") - 1
    sides = ((has_prev, tm - 1), (has_next, tm + 1))

    def target(r):
        return lax.rem(x + lax.div(r, 2), 4) * 2 + lax.rem(half + lax.rem(r, 2), 2)

    def origin(r):
        return lax.rem(x + 4 - lax.div(r, 2), 4) * 2 + lax.rem(half + lax.rem(r, 2), 2)

    def rows_of(s):
        return pl.ds(pl.multiple_of(s * HEAD, HEAD), HEAD)

    def columns_of(s, j):
        return pl.ds(pl.multiple_of((s * HEADS_HERE + j) * HEAD, HEAD), HEAD)

    def head_columns(j):
        return pl.ds(pl.multiple_of(j * HEAD, HEAD), HEAD)

    sources = (video_k, video_v, video_q, video_g)
    landings = (keys, values, queries, grads)
    results = (out_vo, out_vdq, out_vdk, out_vdv)

    def in_copy(j, a, r, sender):
        s = target(r)
        slot = rows_of(me if sender else origin(r))
        index = (j * 4 + a) * 8 + r
        return pltpu.make_async_remote_copy(
            src_ref=sources[a].at[:, columns_of(s, j)],
            dst_ref=landings[a].at[j, slot, :],
            send_sem=in_send.at[index],
            recv_sem=in_recv.at[index],
            device_id=(tm, s),
            device_id_type=MESH,
        )

    def pool_copy(r):
        s = target(r)
        return pltpu.make_async_remote_copy(
            src_ref=pool_stage.at[s],
            dst_ref=pool_land.at[me],
            send_sem=pool_send.at[r],
            recv_sem=pool_recv.at[r],
            device_id=(tm, s),
            device_id_type=MESH,
        )

    def rows_local(a):
        return pltpu.make_async_copy(sources[a], (rows_k, rows_v)[a], local_rows.at[a])

    def in_local(j, a):
        return pltpu.make_async_copy(
            sources[a].at[:, columns_of(me, j)],
            landings[a].at[j, rows_of(me), :],
            local_in.at[j * 4 + a],
        )

    def out_copy(j, a, r, sender):
        s = target(r)
        slot = columns_of(me if sender else origin(r), j)
        index = (j * 4 + a) * 8 + r
        return pltpu.make_async_remote_copy(
            src_ref=video_out.at[a, j, rows_of(s), :],
            dst_ref=results[a].at[:, slot],
            send_sem=out_send.at[index],
            recv_sem=out_recv.at[index],
            device_id=(tm, s),
            device_id_type=MESH,
        )

    def out_local(j, a):
        return pltpu.make_async_copy(
            video_out.at[a, j, rows_of(me), :],
            results[a].at[:, columns_of(me, j)],
            local_out.at[j * 4 + a],
        )

    sound_sources = (audio_k, audio_v, audio_q, audio_g)

    def sound_local(j, a):
        landing = (
            keys.at[j, pl.ds(OWN, AUDIO), :],
            values.at[j, pl.ds(OWN, AUDIO), :],
            sound_q.at[j],
            sound_g.at[j],
        )[a]
        return pltpu.make_async_copy(
            sound_sources[a].at[:, head_columns(j)], landing, local_sound.at[j * 4 + a]
        )

    sound_results = (out_ao, out_adq, out_adk, out_adv)

    def sound_out(j, a):
        return pltpu.make_async_copy(
            audio_out.at[a, j],
            sound_results[a].at[:, head_columns(j)],
            local_sound_out.at[j * 4 + a],
        )

    def near_copy(src, dst, index, device):
        return pltpu.make_async_remote_copy(
            src_ref=src,
            dst_ref=dst,
            send_sem=near_send.at[index],
            recv_sem=near_recv.at[index],
            device_id=(device, me),
            device_id_type=MESH,
        )

    def rim_copy(j, a, d):
        return near_copy(
            rim_out.at[d, a, j],
            (keys, values)[a].at[j, pl.ds((AFTER, BEFORE)[d], CHUNK), :],
            (j * 2 + a) * 2 + d,
            sides[d][1],
        )

    def pooled_copy(j, a, d):
        listed = (keys, values)[a]
        return near_copy(
            listed.at[j, pl.ds(SHARED + POOLED, POOLED), :],
            listed.at[j, pl.ds(SHARED + (2 * POOLED, 0)[d], POOLED), :],
            8 + (j * 2 + a) * 2 + d,
            sides[d][1],
        )

    def pool_grad_copy(j, d):
        return near_copy(
            pool_grad_out.at[d, j], pool_grad_in.at[d, j], 16 + j * 2 + d, sides[d][1]
        )

    def rim_grad_copy(j, d, i):
        a, part = i // 4, pl.ds(i % 4 * POOLED, POOLED)
        return near_copy(
            rim_grad_out.at[d, j, a, part, :],
            rim_grad_in.at[d, j, a, part, :],
            20 + (j * 2 + d) * 8 + i,
            sides[d][1],
        )

    def on_sides(act):
        for d in range(2):

            @pl.when(sides[d][0])
            def _():
                act(d)

    def from_sides(act):
        for d in range(2):

            @pl.when(sides[1 - d][0])
            def _():
                act(d)

    barrier = pltpu.get_barrier_semaphore()

    def greet(r, carry):
        pl.semaphore_signal(barrier, inc=1, device_id=(tm, target(r)), device_id_type=MESH)
        return carry

    lax.fori_loop(1, 8, greet, 0)
    on_sides(
        lambda d: pl.semaphore_signal(
            barrier, inc=1, device_id=(sides[d][1], me), device_id_type=MESH
        )
    )
    for a in range(2):
        rows_local(a).start()
    for j in range(HEADS_HERE):
        for a in range(4):
            sound_local(j, a).start()
    for j in range(HEADS_HERE):
        for a in range(4):
            in_local(j, a).start()

    for j in range(HEADS_HERE):
        for a in range(2):
            sound_local(j, a).wait()

    def stage_rims(d):
        weight = blocks[1 - d, sides[d][1]].astype(F32)
        for j in range(HEADS_HERE):
            for a in range(2):
                listed = (keys, values)[a]
                first = listed[j, OWN : OWN + CHUNK, :].astype(F32)
                second = listed[j, OWN + CHUNK : BEFORE, :].astype(F32)
                rim_out[d, a, j] = (first * (1.0 - weight) + second * weight).astype(BF16)

    on_sides(stage_rims)

    def fill_rims(d):
        spare = jnp.zeros((HEADS_HERE, CHUNK, HEAD), BF16)
        gone = jnp.zeros((HEADS_HERE, POOLED, HEAD), BF16)
        rim_at, pool_at = (AFTER, BEFORE)[d], SHARED + (2 * POOLED, 0)[d]
        for listed in (keys, values):
            listed[:, rim_at : rim_at + CHUNK, :] = spare
            listed[:, pool_at : pool_at + POOLED, :] = gone
        rim_grad_in[d] = jnp.zeros((HEADS_HERE, 2, CHUNK, HEAD), BF16)
        pool_grad_in[d] = jnp.zeros((HEADS_HERE, 2, POOLED, HEAD), BF16)

    for d in range(2):

        @pl.when(jnp.logical_not(sides[1 - d][0]))
        def _():
            fill_rims(d)

    for listed in (keys, values):
        listed[:, SHARED + 3 * POOLED :, :] = jnp.zeros((HEADS_HERE, POOLED, HEAD), BF16)
    member = lax.broadcasted_iota(jnp.int32, (POOL, HEAD), 0)
    group = lax.shift_right_logical(lax.broadcasted_iota(jnp.int32, (POOL, HEAD), 1), 4)
    upper = jnp.where(member == group, 1.0, 0.0).astype(BF16)
    lower = jnp.where(member == group + 8, 1.0, 0.0).astype(BF16)
    for a in range(2):
        rows_local(a).wait()
    for s in range(8):
        for j in range(HEADS_HERE):
            part = slice((s * HEADS_HERE + j) * HEAD, (s * HEADS_HERE + j + 1) * HEAD)
            both = dot(upper, rows_k[:, part]) + dot(lower, rows_v[:, part])
            pool_stage[s, j] = (both * (POOL**-0.5)).astype(BF16)

    pl.semaphore_wait(barrier, 7 + has_prev.astype(jnp.int32) + has_next.astype(jnp.int32))

    def to_peers(act):
        lax.fori_loop(0, 4, lambda i, c: (act(2 * i + 1), c)[1], 0)
        lax.fori_loop(1, 4, lambda i, c: (act(2 * i), c)[1], 0)

    def send_in(j, a):
        to_peers(lambda r: in_copy(j, a, r, True).start())

    def sent_in(j, a):
        to_peers(lambda r: in_copy(j, a, r, True).wait_send())

    def came_in(j, a):
        in_local(j, a).wait()
        to_peers(lambda r: in_copy(j, a, r, False).wait_recv())

    def send_out(j, a):
        out_local(j, a).start()
        to_peers(lambda r: out_copy(j, a, r, True).start())

    def send_rims(j):
        for a in range(2):
            on_sides(lambda d, a=a: rim_copy(j, a, d).start())

    to_peers(lambda r: pool_copy(r).start())
    send_in(0, 0)
    send_in(0, 1)
    send_rims(0)
    pool_land[me] = pool_stage[me]
    to_peers(lambda r: pool_copy(r).wait_recv())
    for j in range(HEADS_HERE):
        landed = [pool_land[s, j].astype(F32) for s in range(8)]
        for a, listed in enumerate((keys, values)):
            pooled = jnp.concatenate([t[a * 8 : a * 8 + 8] for t in landed], axis=0)
            listed[j, SHARED + POOLED : SHARED + 2 * POOLED, :] = pooled.astype(BF16)
            on_sides(lambda d, j=j, a=a: pooled_copy(j, a, d).start())
    send_in(0, 2)
    send_in(0, 3)
    key_sum[...] = jnp.zeros_like(key_sum)
    value_sum[...] = jnp.zeros_like(value_sum)

    live = (rows[0, tm], rows[1, tm])
    place = lax.broadcasted_iota(jnp.int32, (CHUNK, CHUNK), 0)
    first_pooled = jnp.where(has_prev, 0, POOLED)
    last_pooled = jnp.where(has_next, 3 * POOLED, 2 * POOLED)
    video_chunks = tuple(range(8))
    audio_chunks = (4, 5, 8)

    def mask(c, s):
        if c == 6:
            return jnp.where(place < live[0], s, -jnp.inf)
        if c == 7:
            return jnp.where(place < live[1], s, -jnp.inf)
        if c == 8:
            return jnp.where((place >= first_pooled) & (place < last_pooled), s, -jnp.inf)
        return s

    def span(c):
        return slice(c * CHUNK, (c + 1) * CHUNK)

    def attend(j, chunks, q, g):
        top = None
        for i, c in enumerate(chunks):
            s = mask(c, dot(keys[j, span(c), :], q, ((1,), (1,))))
            scores[span(i), :] = s
            peak = jnp.max(s, axis=0, keepdims=True)
            top = peak if top is None else jnp.maximum(top, peak)
        total = jnp.zeros((1, CHUNK), F32)
        for i, c in enumerate(chunks):
            e = jnp.exp2((scores[span(i), :] - top) * (FACTOR * LOG2E))
            scores[span(i), :] = e
            total = total + jnp.sum(e, axis=0, keepdims=True)
        inverse = 1.0 / total
        output = jnp.zeros((HEAD, CHUNK), F32)
        for i, c in enumerate(chunks):
            p = (scores[span(i), :] * inverse).astype(BF16)
            shares[span(i), :] = p
            output = output + dot(values_t[j, :, span(c)], p)
            value_sum[j, span(c), :] += dot(p, g)
        correction = jnp.sum(g.astype(F32).T * output, axis=0, keepdims=True)
        query_grad = jnp.zeros((HEAD, CHUNK), F32)
        for i, c in enumerate(chunks):
            dp = dot(values[j, span(c), :], g, ((1,), (1,)))
            ds = (shares[span(i), :].astype(F32) * (dp - correction) * FACTOR).astype(BF16)
            query_grad = query_grad + dot(keys_t[j, :, span(c)], ds)
            key_sum[j, span(c), :] += dot(ds, q)
        return output.T.astype(BF16), query_grad.T.astype(BF16)

    def finish(j):
        from_sides(lambda d: pool_grad_copy(j, d).wait_recv())
        for a, summed in enumerate((key_sum, value_sum)):
            pooled = summed[j, SHARED + POOLED : SHARED + 2 * POOLED, :]
            for d in range(2):
                pooled = pooled + pool_grad_in[d, j, a].astype(F32)
            pooled = pooled * (POOL**-0.5)
            spread = jnp.broadcast_to(pooled[:, None, :], (POOLED, POOL, HEAD))
            whole = summed[j, :VIDEO, :] + spread.reshape(VIDEO, HEAD)
            video_out[2 + a, j] = whole.astype(BF16)
            send_out(j, 2 + a)

    def turn(j, c):
        keys_t[j, :, span(c)] = keys[j, span(c), :].astype(F32).T.astype(BF16)
        values_t[j, :, span(c)] = values[j, span(c), :].astype(F32).T.astype(BF16)

    def sound(j, carry):
        turn(j, 4)
        turn(j, 5)
        for a in (2, 3):
            sound_local(j, a).wait()
        for a in range(2):
            from_sides(lambda d, a=a: pooled_copy(j, a, d).wait_recv())
        turn(j, 8)

        def step(i, c):
            part = pl.ds(pl.multiple_of(i * CHUNK, CHUNK), CHUNK)
            o, dq = attend(j, audio_chunks, sound_q[j, part, :], sound_g[j, part, :])
            audio_out[0, j, part, :] = o
            audio_out[1, j, part, :] = dq
            return c

        lax.fori_loop(0, AUDIO // CHUNK, step, 0)
        for d in range(2):
            at = SHARED + (0, 2 * POOLED)[d]
            pool_grad_out[d, j, 0] = key_sum[j, at : at + POOLED, :].astype(BF16)
            pool_grad_out[d, j, 1] = value_sum[j, at : at + POOLED, :].astype(BF16)
        on_sides(lambda d: pool_grad_copy(j, d).start())
        sound_out(j, 0).start()
        sound_out(j, 1).start()

        @pl.when(j == 0)
        def _():
            send_in(1, 0)
            send_in(1, 1)
            send_rims(1)

        return carry

    lax.fori_loop(0, HEADS_HERE, sound, 0)
    send_in(1, 2)
    send_in(1, 3)

    def video(j, carry):
        for a in range(2):
            from_sides(lambda d, a=a: rim_copy(j, a, d).wait_recv())
            came_in(j, a)
        for c in (0, 1, 2, 3, 6, 7):
            turn(j, c)
        came_in(j, 2)
        came_in(j, 3)

        def step(k, c):
            i = lax.rem(x + k, 4)
            part = pl.ds(pl.multiple_of(i * CHUNK, CHUNK), CHUNK)
            o, dq = attend(j, video_chunks, queries[j, part, :], grads[j, part, :])
            video_out[0, j, part, :] = o
            video_out[1, j, part, :] = dq
            return c

        lax.fori_loop(0, 4, step, 0)
        for d in range(2):
            at = (BEFORE, AFTER)[d]
            rim_grad_out[d, j, 0] = key_sum[j, at : at + CHUNK, :].astype(BF16)
            rim_grad_out[d, j, 1] = value_sum[j, at : at + CHUNK, :].astype(BF16)
        for i in range(8):
            on_sides(lambda d, i=i: rim_grad_copy(j, d, i).start())
        send_out(j, 0)
        send_out(j, 1)
        finish(j)
        return carry

    lax.fori_loop(0, HEADS_HERE, video, 0)

    prev_weight = blocks[1, jnp.maximum(tm - 1, 0)].astype(F32)
    next_weight = blocks[0, jnp.minimum(tm + 1, lax.axis_size("tm") - 1)].astype(F32)
    weights = (next_weight, prev_weight)
    for j in range(HEADS_HERE):
        for i in range(8):
            from_sides(lambda d, j=j, i=i: rim_grad_copy(j, d, i).wait_recv())
        for a in range(2):
            for b in range(2):
                part = slice(b * CHUNK, (b + 1) * CHUNK)
                whole = (key_sum, value_sum)[a][j, OWN + b * CHUNK : OWN + (b + 1) * CHUNK, :]
                for d in range(2):
                    weight = weights[d] if b else 1.0 - weights[d]
                    whole = whole + rim_grad_in[d, j, a].astype(F32) * weight
                audio_out[2 + a, j, part, :] = whole.astype(BF16)
            sound_out(j, 2 + a).start()

    for j in range(HEADS_HERE):
        for a in range(4):
            sound_out(j, a).wait()
            out_local(j, a).wait()
            to_peers(lambda r, j=j, a=a: out_copy(j, a, r, True).wait_send())
            to_peers(lambda r, j=j, a=a: out_copy(j, a, r, False).wait_recv())
        for a in range(2):
            on_sides(lambda d, j=j, a=a: rim_copy(j, a, d).wait_send())
            on_sides(lambda d, j=j, a=a: pooled_copy(j, a, d).wait_send())
        on_sides(lambda d, j=j: pool_grad_copy(j, d).wait_send())
        for i in range(8):
            on_sides(lambda d, j=j, i=i: rim_grad_copy(j, d, i).wait_send())
    for j in range(HEADS_HERE):
        for a in range(4):
            sent_in(j, a)
    to_peers(lambda r: pool_copy(r).wait_send())


def publish(*refs):
    made, final, held, sem = refs[:8], refs[8:16], refs[16:24], refs[24]
    reads = [pltpu.make_async_copy(made[i], held[i], sem.at[i]) for i in range(8)]
    writes = [pltpu.make_async_copy(held[i], final[i], sem.at[8 + i]) for i in range(8)]
    for read in reads:
        read.start()
    for read, write in zip(reads, writes):
        read.wait()
        write.start()
    for write in writes:
        write.wait()


def per_device(*args):
    video = jax.ShapeDtypeStruct(args[0].shape, BF16)
    audio = jax.ShapeDtypeStruct(args[4].shape, BF16)
    two = HEADS_HERE
    made = pl.pallas_call(
        kernel,
        out_shape=(video,) * 4 + (audio,) * 4,
        in_specs=[pl.BlockSpec(memory_space=pltpu.HBM)] * 8
        + [pl.BlockSpec(memory_space=pltpu.SMEM)] * 2,
        out_specs=(pl.BlockSpec(memory_space=pl.ANY),) * 8,
        scratch_shapes=[
            pltpu.VMEM((two, LISTED, HEAD), BF16),
            pltpu.VMEM((two, LISTED, HEAD), BF16),
            pltpu.VMEM((two, VIDEO, HEAD), BF16),
            pltpu.VMEM((two, VIDEO, HEAD), BF16),
            pltpu.VMEM((two, AUDIO, HEAD), BF16),
            pltpu.VMEM((two, AUDIO, HEAD), BF16),
            pltpu.VMEM((two, HEAD, LISTED), BF16),
            pltpu.VMEM((two, HEAD, LISTED), BF16),
            pltpu.VMEM((two, LISTED, HEAD), F32),
            pltpu.VMEM((two, LISTED, HEAD), F32),
            pltpu.VMEM((SHARED, CHUNK), F32),
            pltpu.VMEM((SHARED, CHUNK), BF16),
            pltpu.VMEM((HEAD, 8 * two * HEAD), BF16),
            pltpu.VMEM((HEAD, 8 * two * HEAD), BF16),
            pltpu.VMEM((8, two, POOL, HEAD), BF16),
            pltpu.VMEM((8, two, POOL, HEAD), BF16),
            pltpu.VMEM((4, two, VIDEO, HEAD), BF16),
            pltpu.VMEM((4, two, AUDIO, HEAD), BF16),
            pltpu.VMEM((2, 2, two, CHUNK, HEAD), BF16),
            pltpu.VMEM((2, two, 2, CHUNK, HEAD), BF16),
            pltpu.VMEM((2, two, 2, CHUNK, HEAD), BF16),
            pltpu.VMEM((2, two, 2, POOLED, HEAD), BF16),
            pltpu.VMEM((2, two, 2, POOLED, HEAD), BF16),
            pltpu.SemaphoreType.DMA((64,)),
            pltpu.SemaphoreType.DMA((64,)),
            pltpu.SemaphoreType.DMA((64,)),
            pltpu.SemaphoreType.DMA((64,)),
            pltpu.SemaphoreType.DMA((52,)),
            pltpu.SemaphoreType.DMA((52,)),
            pltpu.SemaphoreType.DMA((8,)),
            pltpu.SemaphoreType.DMA((8,)),
            pltpu.SemaphoreType.DMA((2,)),
            pltpu.SemaphoreType.DMA((8,)),
            pltpu.SemaphoreType.DMA((8,)),
            pltpu.SemaphoreType.DMA((8,)),
            pltpu.SemaphoreType.DMA((8,)),
        ],
        compiler_params=pltpu.CompilerParams(
            collective_id=0, has_side_effects=True, vmem_limit_bytes=60 * 1024 * 1024
        ),
        name="joint_attention",
    )(*args[:8], args[8].T, args[9].T)
    return pl.pallas_call(
        publish,
        out_shape=(video,) * 4 + (audio,) * 4,
        in_specs=[pl.BlockSpec(memory_space=pl.ANY)] * 8,
        out_specs=(pl.BlockSpec(memory_space=pltpu.HBM),) * 8,
        scratch_shapes=[pltpu.VMEM(args[0].shape, BF16)] * 4
        + [pltpu.VMEM(args[4].shape, BF16)] * 4
        + [pltpu.SemaphoreType.DMA((16,))],
        name="publish",
    )(*made)


def solution(mesh):
    tokens, sound = P(("tm", "space"), None), P("tm", "space")
    return jax.shard_map(
        per_device,
        mesh=mesh,
        in_specs=(tokens,) * 4 + (sound,) * 4 + (P(), P()),
        out_specs=(tokens,) * 4 + (sound,) * 4,
        check_vma=False,
    )
```

```python
import jax
import jax.numpy as jnp
from jax import lax
from jax.experimental import pallas as pl
from jax.experimental.pallas import tpu as pltpu
from jax.sharding import PartitionSpec as P

HEAD = 128
CHUNK = 256
POOL = 16
HEADS_HERE = 2
RUN = 8
VIDEO = 1024
AUDIO = 512
POOLED = 64
OWN = VIDEO
BEFORE = VIDEO + AUDIO
AFTER = BEFORE + CHUNK
SHARED = AFTER + CHUNK
LISTED = SHARED + CHUNK
FACTOR = HEAD**-0.5
LOG2E = 1.4426950408889634
MESH = pl.DeviceIdType.MESH
F32 = jnp.float32
BF16 = jnp.bfloat16


def dot(a, b, contract=((1,), (0,))):
    return lax.dot_general(a, b, (contract, ((), ())), preferred_element_type=F32)


def kernel(
    video_q,
    video_k,
    video_v,
    video_g,
    audio_q,
    audio_k,
    audio_v,
    audio_g,
    blocks,
    rows,
    out_vo,
    out_vdq,
    out_vdk,
    out_vdv,
    out_ao,
    out_adq,
    out_adk,
    out_adv,
    keys,
    values,
    queries,
    grads,
    sound_q,
    sound_g,
    keys_t,
    values_t,
    key_sum,
    value_sum,
    scores,
    shares,
    rows_k,
    rows_v,
    pool_stage,
    pool_land,
    video_out,
    audio_out,
    rim_out,
    relay_in,
    rim_grad_out,
    rim_grad_in,
    pool_grad_out,
    pool_grad_in,
    in_send,
    in_recv,
    out_send,
    out_recv,
    near_send,
    near_recv,
    pool_send,
    pool_recv,
    relay_recv,
    onward_send,
    local_rows,
    local_in,
    local_sound,
    local_out,
    local_sound_out,
):
    tm = lax.axis_index("tm")
    me = lax.axis_index("space")
    x, half = lax.div(me, 2), lax.rem(me, 2)
    has_prev, has_next = tm > 0, tm < lax.axis_size("tm") - 1
    sides = ((has_prev, tm - 1), (has_next, tm + 1))
    place_in_run = lax.rem(tm, RUN)
    run_ends = (place_in_run == 0, place_in_run == RUN - 1)
    at_end = run_ends[0] | run_ends[1]
    other_end = jnp.where(run_ends[0], tm + RUN - 1, tm - RUN + 1)
    run_below, run_above = tm >= RUN, tm < lax.axis_size("tm") - RUN
    onward = ((run_ends[1] & run_below, tm - RUN), (run_ends[0] & run_above, tm + RUN))

    def target(r):
        return lax.rem(x + lax.div(r, 2), 4) * 2 + lax.rem(half + lax.rem(r, 2), 2)

    def origin(r):
        return lax.rem(x + 4 - lax.div(r, 2), 4) * 2 + lax.rem(half + lax.rem(r, 2), 2)

    def rows_of(s):
        return pl.ds(pl.multiple_of(s * HEAD, HEAD), HEAD)

    def columns_of(s, j):
        return pl.ds(pl.multiple_of((s * HEADS_HERE + j) * HEAD, HEAD), HEAD)

    def head_columns(j):
        return pl.ds(pl.multiple_of(j * HEAD, HEAD), HEAD)

    sources = (video_k, video_v, video_q, video_g)
    landings = (keys, values, queries, grads)
    results = (out_vo, out_vdq, out_vdk, out_vdv)

    def in_copy(j, a, r, sender):
        s = target(r)
        slot = rows_of(me if sender else origin(r))
        index = (j * 4 + a) * 8 + r
        return pltpu.make_async_remote_copy(
            src_ref=sources[a].at[:, columns_of(s, j)],
            dst_ref=landings[a].at[j, slot, :],
            send_sem=in_send.at[index],
            recv_sem=in_recv.at[index],
            device_id=(tm, s),
            device_id_type=MESH,
        )

    def pool_copy(r):
        s = target(r)
        return pltpu.make_async_remote_copy(
            src_ref=pool_stage.at[s],
            dst_ref=pool_land.at[me],
            send_sem=pool_send.at[r],
            recv_sem=pool_recv.at[r],
            device_id=(tm, s),
            device_id_type=MESH,
        )

    def rows_local(a):
        return pltpu.make_async_copy(sources[a], (rows_k, rows_v)[a], local_rows.at[a])

    def in_local(j, a):
        return pltpu.make_async_copy(
            sources[a].at[:, columns_of(me, j)],
            landings[a].at[j, rows_of(me), :],
            local_in.at[j * 4 + a],
        )

    def out_copy(j, a, r, sender):
        s = target(r)
        slot = columns_of(me if sender else origin(r), j)
        index = (j * 4 + a) * 8 + r
        return pltpu.make_async_remote_copy(
            src_ref=video_out.at[a, j, rows_of(s), :],
            dst_ref=results[a].at[:, slot],
            send_sem=out_send.at[index],
            recv_sem=out_recv.at[index],
            device_id=(tm, s),
            device_id_type=MESH,
        )

    def out_local(j, a):
        return pltpu.make_async_copy(
            video_out.at[a, j, rows_of(me), :],
            results[a].at[:, columns_of(me, j)],
            local_out.at[j * 4 + a],
        )

    sound_sources = (audio_k, audio_v, audio_q, audio_g)

    def sound_local(j, a):
        landing = (
            keys.at[j, pl.ds(OWN, AUDIO), :],
            values.at[j, pl.ds(OWN, AUDIO), :],
            sound_q.at[j],
            sound_g.at[j],
        )[a]
        return pltpu.make_async_copy(
            sound_sources[a].at[:, head_columns(j)], landing, local_sound.at[j * 4 + a]
        )

    sound_results = (out_ao, out_adq, out_adk, out_adv)

    def sound_out(j, a):
        return pltpu.make_async_copy(
            audio_out.at[a, j],
            sound_results[a].at[:, head_columns(j)],
            local_sound_out.at[j * 4 + a],
        )

    def near_copy(src, dst, index, device):
        return pltpu.make_async_remote_copy(
            src_ref=src,
            dst_ref=dst,
            send_sem=near_send.at[index],
            recv_sem=near_recv.at[index],
            device_id=(device, me),
            device_id_type=MESH,
        )

    def rim_copy(j, a, d):
        return near_copy(
            rim_out.at[d, a, j],
            (keys, values)[a].at[j, pl.ds((AFTER, BEFORE)[d], CHUNK), :],
            (j * 2 + a) * 2 + d,
            sides[d][1],
        )

    def relay_copy(j, a, d):
        return pltpu.make_async_remote_copy(
            src_ref=rim_out.at[d, a, j],
            dst_ref=relay_in.at[j, a],
            send_sem=near_send.at[(j * 2 + a) * 2 + d],
            recv_sem=relay_recv.at[j * 2 + a],
            device_id=(other_end, me),
            device_id_type=MESH,
        )

    def onward_copy(j, a, d):
        return pltpu.make_async_remote_copy(
            src_ref=relay_in.at[j, a],
            dst_ref=(keys, values)[a].at[j, pl.ds((AFTER, BEFORE)[d], CHUNK), :],
            send_sem=onward_send.at[j * 2 + a],
            recv_sem=near_recv.at[(j * 2 + a) * 2 + d],
            device_id=(onward[d][1], me),
            device_id_type=MESH,
        )

    def pooled_copy(j, a, d):
        listed = (keys, values)[a]
        return near_copy(
            listed.at[j, pl.ds(SHARED + POOLED, POOLED), :],
            listed.at[j, pl.ds(SHARED + (2 * POOLED, 0)[d], POOLED), :],
            8 + (j * 2 + a) * 2 + d,
            sides[d][1],
        )

    def pool_grad_copy(j, d):
        return near_copy(
            pool_grad_out.at[d, j], pool_grad_in.at[d, j], 16 + j * 2 + d, sides[d][1]
        )

    def rim_grad_copy(j, d, i):
        a, part = i // 4, pl.ds(i % 4 * POOLED, POOLED)
        return near_copy(
            rim_grad_out.at[d, j, a, part, :],
            rim_grad_in.at[d, j, a, part, :],
            20 + (j * 2 + d) * 8 + i,
            sides[d][1],
        )

    def on_sides(act):
        for d in range(2):

            @pl.when(sides[d][0])
            def _():
                act(d)

    def from_sides(act):
        for d in range(2):

            @pl.when(sides[1 - d][0])
            def _():
                act(d)

    barrier = pltpu.get_barrier_semaphore()

    def greet(r, carry):
        pl.semaphore_signal(barrier, inc=1, device_id=(tm, target(r)), device_id_type=MESH)
        return carry

    lax.fori_loop(1, 8, greet, 0)
    on_sides(
        lambda d: pl.semaphore_signal(
            barrier, inc=1, device_id=(sides[d][1], me), device_id_type=MESH
        )
    )
    for there, device in (
        (at_end, other_end),
        (at_end & run_below, tm - RUN),
        (at_end & run_above, tm + RUN),
    ):

        @pl.when(there)
        def _(device=device):
            pl.semaphore_signal(barrier, inc=1, device_id=(device, me), device_id_type=MESH)

    for a in range(2):
        rows_local(a).start()
    for j in range(HEADS_HERE):
        for a in range(4):
            sound_local(j, a).start()
    for j in range(HEADS_HERE):
        for a in range(4):
            in_local(j, a).start()

    for j in range(HEADS_HERE):
        for a in range(2):
            sound_local(j, a).wait()

    def stage_rims(d):
        weight = blocks[1 - d, sides[d][1]].astype(F32)
        for j in range(HEADS_HERE):
            for a in range(2):
                listed = (keys, values)[a]
                first = listed[j, OWN : OWN + CHUNK, :].astype(F32)
                second = listed[j, OWN + CHUNK : BEFORE, :].astype(F32)
                rim_out[d, a, j] = (first * (1.0 - weight) + second * weight).astype(BF16)

    on_sides(stage_rims)

    def fill_rims(d):
        spare = jnp.zeros((HEADS_HERE, CHUNK, HEAD), BF16)
        gone = jnp.zeros((HEADS_HERE, POOLED, HEAD), BF16)
        rim_at, pool_at = (AFTER, BEFORE)[d], SHARED + (2 * POOLED, 0)[d]
        for listed in (keys, values):
            listed[:, rim_at : rim_at + CHUNK, :] = spare
            listed[:, pool_at : pool_at + POOLED, :] = gone
        rim_grad_in[d] = jnp.zeros((HEADS_HERE, 2, CHUNK, HEAD), BF16)
        pool_grad_in[d] = jnp.zeros((HEADS_HERE, 2, POOLED, HEAD), BF16)

    for d in range(2):

        @pl.when(jnp.logical_not(sides[1 - d][0]))
        def _():
            fill_rims(d)

    for listed in (keys, values):
        listed[:, SHARED + 3 * POOLED :, :] = jnp.zeros((HEADS_HERE, POOLED, HEAD), BF16)
    member = lax.broadcasted_iota(jnp.int32, (POOL, HEAD), 0)
    group = lax.shift_right_logical(lax.broadcasted_iota(jnp.int32, (POOL, HEAD), 1), 4)
    upper = jnp.where(member == group, 1.0, 0.0).astype(BF16)
    lower = jnp.where(member == group + 8, 1.0, 0.0).astype(BF16)
    for a in range(2):
        rows_local(a).wait()
    for s in range(8):
        for j in range(HEADS_HERE):
            part = slice((s * HEADS_HERE + j) * HEAD, (s * HEADS_HERE + j + 1) * HEAD)
            both = dot(upper, rows_k[:, part]) + dot(lower, rows_v[:, part])
            pool_stage[s, j] = (both * (POOL**-0.5)).astype(BF16)

    one = jnp.int32(1)
    greeted = 7 + jnp.where(has_prev, one, 0) + jnp.where(has_next, one, 0)
    ends = one + jnp.where(run_below, one, 0) + jnp.where(run_above, one, 0)
    pl.semaphore_wait(barrier, greeted + jnp.where(at_end, ends, 0))

    def to_peers(act):
        lax.fori_loop(0, 4, lambda i, c: (act(2 * i + 1), c)[1], 0)
        lax.fori_loop(1, 4, lambda i, c: (act(2 * i), c)[1], 0)

    def send_in(j, a):
        to_peers(lambda r: in_copy(j, a, r, True).start())

    def sent_in(j, a):
        to_peers(lambda r: in_copy(j, a, r, True).wait_send())

    def came_in(j, a):
        in_local(j, a).wait()
        to_peers(lambda r: in_copy(j, a, r, False).wait_recv())

    def send_out(j, a):
        out_local(j, a).start()
        to_peers(lambda r: out_copy(j, a, r, True).start())

    def send_rims(j):
        def start(a, d):
            @pl.when(run_ends[d])
            def _():
                relay_copy(j, a, d).start()

            @pl.when(jnp.logical_not(run_ends[d]))
            def _():
                rim_copy(j, a, d).start()

        for a in range(2):
            on_sides(lambda d, a=a: start(a, d))

    def pass_on(j):
        for d in range(2):

            @pl.when(onward[d][0])
            def _(d=d):
                for a in range(2):
                    relay_copy(j, a, d).wait_recv()
                    onward_copy(j, a, d).start()

    send_rims(0)
    send_rims(1)
    to_peers(lambda r: pool_copy(r).start())
    send_in(0, 0)
    pass_on(0)
    send_in(0, 1)
    pass_on(1)
    pool_land[me] = pool_stage[me]
    to_peers(lambda r: pool_copy(r).wait_recv())
    for j in range(HEADS_HERE):
        landed = [pool_land[s, j].astype(F32) for s in range(8)]
        for a, listed in enumerate((keys, values)):
            pooled = jnp.concatenate([t[a * 8 : a * 8 + 8] for t in landed], axis=0)
            listed[j, SHARED + POOLED : SHARED + 2 * POOLED, :] = pooled.astype(BF16)
            on_sides(lambda d, j=j, a=a: pooled_copy(j, a, d).start())
    send_in(0, 2)
    send_in(0, 3)
    key_sum[...] = jnp.zeros_like(key_sum)
    value_sum[...] = jnp.zeros_like(value_sum)

    live = (rows[0, tm], rows[1, tm])
    place = lax.broadcasted_iota(jnp.int32, (CHUNK, CHUNK), 0)
    first_pooled = jnp.where(has_prev, 0, POOLED)
    last_pooled = jnp.where(has_next, 3 * POOLED, 2 * POOLED)
    video_chunks = tuple(range(8))
    audio_chunks = (4, 5, 8)

    def mask(c, s):
        if c == 6:
            return jnp.where(place < live[0], s, -jnp.inf)
        if c == 7:
            return jnp.where(place < live[1], s, -jnp.inf)
        if c == 8:
            return jnp.where((place >= first_pooled) & (place < last_pooled), s, -jnp.inf)
        return s

    def span(c):
        return slice(c * CHUNK, (c + 1) * CHUNK)

    def attend(j, chunks, q, g):
        top = None
        for i, c in enumerate(chunks):
            s = mask(c, dot(keys[j, span(c), :], q, ((1,), (1,))))
            scores[span(i), :] = s
            peak = jnp.max(s, axis=0, keepdims=True)
            top = peak if top is None else jnp.maximum(top, peak)
        total = jnp.zeros((1, CHUNK), F32)
        for i, c in enumerate(chunks):
            e = jnp.exp2((scores[span(i), :] - top) * (FACTOR * LOG2E))
            scores[span(i), :] = e
            total = total + jnp.sum(e, axis=0, keepdims=True)
        inverse = 1.0 / total
        output = jnp.zeros((HEAD, CHUNK), F32)
        for i, c in enumerate(chunks):
            p = (scores[span(i), :] * inverse).astype(BF16)
            shares[span(i), :] = p
            output = output + dot(values_t[j, :, span(c)], p)
            value_sum[j, span(c), :] += dot(p, g)
        correction = jnp.sum(g.astype(F32).T * output, axis=0, keepdims=True)
        query_grad = jnp.zeros((HEAD, CHUNK), F32)
        for i, c in enumerate(chunks):
            dp = dot(values[j, span(c), :], g, ((1,), (1,)))
            ds = (shares[span(i), :].astype(F32) * (dp - correction) * FACTOR).astype(BF16)
            query_grad = query_grad + dot(keys_t[j, :, span(c)], ds)
            key_sum[j, span(c), :] += dot(ds, q)
        return output.T.astype(BF16), query_grad.T.astype(BF16)

    def finish(j):
        from_sides(lambda d: pool_grad_copy(j, d).wait_recv())
        for a, summed in enumerate((key_sum, value_sum)):
            pooled = summed[j, SHARED + POOLED : SHARED + 2 * POOLED, :]
            for d in range(2):
                pooled = pooled + pool_grad_in[d, j, a].astype(F32)
            pooled = pooled * (POOL**-0.5)
            spread = jnp.broadcast_to(pooled[:, None, :], (POOLED, POOL, HEAD))
            whole = summed[j, :VIDEO, :] + spread.reshape(VIDEO, HEAD)
            video_out[2 + a, j] = whole.astype(BF16)
            send_out(j, 2 + a)

    def turn(j, c):
        keys_t[j, :, span(c)] = keys[j, span(c), :].astype(F32).T.astype(BF16)
        values_t[j, :, span(c)] = values[j, span(c), :].astype(F32).T.astype(BF16)

    def sound(j, carry):
        turn(j, 4)
        turn(j, 5)
        for a in (2, 3):
            sound_local(j, a).wait()
        for a in range(2):
            from_sides(lambda d, a=a: pooled_copy(j, a, d).wait_recv())
        turn(j, 8)

        def step(i, c):
            part = pl.ds(pl.multiple_of(i * CHUNK, CHUNK), CHUNK)
            o, dq = attend(j, audio_chunks, sound_q[j, part, :], sound_g[j, part, :])
            audio_out[0, j, part, :] = o
            audio_out[1, j, part, :] = dq
            return c

        lax.fori_loop(0, AUDIO // CHUNK, step, 0)
        for d in range(2):
            at = SHARED + (0, 2 * POOLED)[d]
            pool_grad_out[d, j, 0] = key_sum[j, at : at + POOLED, :].astype(BF16)
            pool_grad_out[d, j, 1] = value_sum[j, at : at + POOLED, :].astype(BF16)
        on_sides(lambda d: pool_grad_copy(j, d).start())
        sound_out(j, 0).start()
        sound_out(j, 1).start()

        @pl.when(j == 0)
        def _():
            send_in(1, 0)
            send_in(1, 1)

        return carry

    lax.fori_loop(0, HEADS_HERE, sound, 0)
    send_in(1, 2)
    send_in(1, 3)

    def video(j, carry):
        for a in range(2):
            from_sides(lambda d, a=a: rim_copy(j, a, d).wait_recv())
            came_in(j, a)
        for c in (0, 1, 2, 3, 6, 7):
            turn(j, c)
        came_in(j, 2)
        came_in(j, 3)

        def step(k, c):
            i = lax.rem(x + k, 4)
            part = pl.ds(pl.multiple_of(i * CHUNK, CHUNK), CHUNK)
            o, dq = attend(j, video_chunks, queries[j, part, :], grads[j, part, :])
            video_out[0, j, part, :] = o
            video_out[1, j, part, :] = dq
            for a in range(2):
                out_copy(j, a, 2 * k + 1, True).start()

                @pl.when(k == 0)
                def _(a=a):
                    out_local(j, a).start()

                @pl.when(k > 0)
                def _(a=a):
                    out_copy(j, a, 2 * k, True).start()

            return c

        lax.fori_loop(0, 4, step, 0)
        for d in range(2):
            at = (BEFORE, AFTER)[d]
            rim_grad_out[d, j, 0] = key_sum[j, at : at + CHUNK, :].astype(BF16)
            rim_grad_out[d, j, 1] = value_sum[j, at : at + CHUNK, :].astype(BF16)
        for i in range(8):
            on_sides(lambda d, i=i: rim_grad_copy(j, d, i).start())
        finish(j)
        return carry

    lax.fori_loop(0, HEADS_HERE, video, 0)

    prev_weight = blocks[1, jnp.maximum(tm - 1, 0)].astype(F32)
    next_weight = blocks[0, jnp.minimum(tm + 1, lax.axis_size("tm") - 1)].astype(F32)
    weights = (next_weight, prev_weight)
    for j in range(HEADS_HERE):
        for i in range(8):
            from_sides(lambda d, j=j, i=i: rim_grad_copy(j, d, i).wait_recv())
        for a in range(2):
            for b in range(2):
                part = slice(b * CHUNK, (b + 1) * CHUNK)
                whole = (key_sum, value_sum)[a][j, OWN + b * CHUNK : OWN + (b + 1) * CHUNK, :]
                for d in range(2):
                    weight = weights[d] if b else 1.0 - weights[d]
                    whole = whole + rim_grad_in[d, j, a].astype(F32) * weight
                audio_out[2 + a, j, part, :] = whole.astype(BF16)
            sound_out(j, 2 + a).start()

    for j in range(HEADS_HERE):
        for a in range(4):
            sound_out(j, a).wait()
            out_local(j, a).wait()
            to_peers(lambda r, j=j, a=a: out_copy(j, a, r, True).wait_send())
            to_peers(lambda r, j=j, a=a: out_copy(j, a, r, False).wait_recv())
        for a in range(2):
            on_sides(lambda d, j=j, a=a: rim_copy(j, a, d).wait_send())
            on_sides(lambda d, j=j, a=a: pooled_copy(j, a, d).wait_send())
        on_sides(lambda d, j=j: pool_grad_copy(j, d).wait_send())
        for i in range(8):
            on_sides(lambda d, j=j, i=i: rim_grad_copy(j, d, i).wait_send())
    for j in range(HEADS_HERE):
        for a in range(4):
            sent_in(j, a)
    to_peers(lambda r: pool_copy(r).wait_send())
    for d in range(2):

        @pl.when(onward[d][0])
        def _(d=d):
            for j in range(HEADS_HERE):
                for a in range(2):
                    onward_copy(j, a, d).wait_send()


def publish(*refs):
    sem = refs[16]
    copies = [pltpu.make_async_copy(refs[i], refs[8 + i], sem.at[i]) for i in range(8)]
    for copy in copies:
        copy.start()
    for copy in copies:
        copy.wait()


def per_device(*args):
    video = jax.ShapeDtypeStruct(args[0].shape, BF16)
    audio = jax.ShapeDtypeStruct(args[4].shape, BF16)
    two = HEADS_HERE
    made = pl.pallas_call(
        kernel,
        out_shape=(pltpu.VMEM(video.shape, BF16),) * 4 + (pltpu.VMEM(audio.shape, BF16),) * 4,
        in_specs=[pl.BlockSpec(memory_space=pltpu.HBM)] * 8
        + [pl.BlockSpec(memory_space=pltpu.SMEM)] * 2,
        out_specs=(pl.BlockSpec(memory_space=pltpu.VMEM),) * 8,
        scratch_shapes=[
            pltpu.VMEM((two, LISTED, HEAD), BF16),
            pltpu.VMEM((two, LISTED, HEAD), BF16),
            pltpu.VMEM((two, VIDEO, HEAD), BF16),
            pltpu.VMEM((two, VIDEO, HEAD), BF16),
            pltpu.VMEM((two, AUDIO, HEAD), BF16),
            pltpu.VMEM((two, AUDIO, HEAD), BF16),
            pltpu.VMEM((two, HEAD, LISTED), BF16),
            pltpu.VMEM((two, HEAD, LISTED), BF16),
            pltpu.VMEM((two, LISTED, HEAD), F32),
            pltpu.VMEM((two, LISTED, HEAD), F32),
            pltpu.VMEM((SHARED, CHUNK), F32),
            pltpu.VMEM((SHARED, CHUNK), BF16),
            pltpu.VMEM((HEAD, 8 * two * HEAD), BF16),
            pltpu.VMEM((HEAD, 8 * two * HEAD), BF16),
            pltpu.VMEM((8, two, POOL, HEAD), BF16),
            pltpu.VMEM((8, two, POOL, HEAD), BF16),
            pltpu.VMEM((4, two, VIDEO, HEAD), BF16),
            pltpu.VMEM((4, two, AUDIO, HEAD), BF16),
            pltpu.VMEM((2, 2, two, CHUNK, HEAD), BF16),
            pltpu.VMEM((two, 2, CHUNK, HEAD), BF16),
            pltpu.VMEM((2, two, 2, CHUNK, HEAD), BF16),
            pltpu.VMEM((2, two, 2, CHUNK, HEAD), BF16),
            pltpu.VMEM((2, two, 2, POOLED, HEAD), BF16),
            pltpu.VMEM((2, two, 2, POOLED, HEAD), BF16),
            pltpu.SemaphoreType.DMA((64,)),
            pltpu.SemaphoreType.DMA((64,)),
            pltpu.SemaphoreType.DMA((64,)),
            pltpu.SemaphoreType.DMA((64,)),
            pltpu.SemaphoreType.DMA((52,)),
            pltpu.SemaphoreType.DMA((52,)),
            pltpu.SemaphoreType.DMA((8,)),
            pltpu.SemaphoreType.DMA((8,)),
            pltpu.SemaphoreType.DMA((4,)),
            pltpu.SemaphoreType.DMA((4,)),
            pltpu.SemaphoreType.DMA((2,)),
            pltpu.SemaphoreType.DMA((8,)),
            pltpu.SemaphoreType.DMA((8,)),
            pltpu.SemaphoreType.DMA((8,)),
            pltpu.SemaphoreType.DMA((8,)),
        ],
        compiler_params=pltpu.CompilerParams(
            collective_id=0, has_side_effects=True, vmem_limit_bytes=60 * 1024 * 1024
        ),
        name="joint_attention",
    )(*args[:8], args[8].T, args[9].T)
    return pl.pallas_call(
        publish,
        out_shape=(video,) * 4 + (audio,) * 4,
        in_specs=[pl.BlockSpec(memory_space=pl.ANY)] * 8,
        out_specs=(pl.BlockSpec(memory_space=pltpu.HBM),) * 8,
        scratch_shapes=[pltpu.SemaphoreType.DMA((8,))],
        compiler_params=pltpu.CompilerParams(vmem_limit_bytes=1024 * 1024),
        name="publish",
    )(*made)


def solution(mesh):
    tokens, sound = P(("tm", "space"), None), P("tm", "space")
    return jax.shard_map(
        per_device,
        mesh=mesh,
        in_specs=(tokens,) * 4 + (sound,) * 4 + (P(), P()),
        out_specs=(tokens,) * 4 + (sound,) * 4,
        check_vma=False,
    )
```

```python
import jax
import jax.numpy as jnp
from jax import lax
from jax.experimental import pallas as pl
from jax.experimental.pallas import tpu as pltpu
from jax.sharding import PartitionSpec as P

HEAD = 128
CHUNK = 256
POOL = 16
HEADS_HERE = 2
RUN = 8
VIDEO = 1024
AUDIO = 512
POOLED = 64
OWN = VIDEO
BEFORE = VIDEO + AUDIO
AFTER = BEFORE + CHUNK
SHARED = AFTER + CHUNK
LISTED = SHARED + CHUNK
FACTOR = HEAD**-0.5
LOG2E = 1.4426950408889634
MESH = pl.DeviceIdType.MESH
F32 = jnp.float32
BF16 = jnp.bfloat16


def dot(a, b, contract=((1,), (0,))):
    return lax.dot_general(a, b, (contract, ((), ())), preferred_element_type=F32)


def kernel(
    video_q,
    video_k,
    video_v,
    video_g,
    audio_q,
    audio_k,
    audio_v,
    audio_g,
    blocks,
    rows,
    out_vo,
    out_vdq,
    out_vdk,
    out_vdv,
    out_ao,
    out_adq,
    out_adk,
    out_adv,
    keys,
    values,
    queries,
    grads,
    sound_q,
    sound_g,
    keys_t,
    values_t,
    key_sum,
    value_sum,
    scores,
    shares,
    rows_k,
    rows_v,
    pool_stage,
    pool_land,
    video_out,
    audio_out,
    rim_out,
    relay_in,
    rim_grad_out,
    rim_grad_in,
    pool_grad_out,
    pool_grad_in,
    in_send,
    in_recv,
    out_send,
    out_recv,
    near_send,
    near_recv,
    pool_send,
    pool_recv,
    relay_recv,
    onward_send,
    local_rows,
    local_in,
    local_sound,
    local_out,
    local_sound_out,
):
    tm = lax.axis_index("tm")
    me = lax.axis_index("space")
    x, half = lax.div(me, 2), lax.rem(me, 2)
    has_prev, has_next = tm > 0, tm < lax.axis_size("tm") - 1
    sides = ((has_prev, tm - 1), (has_next, tm + 1))
    place_in_run = lax.rem(tm, RUN)
    run_ends = (place_in_run == 0, place_in_run == RUN - 1)
    at_end = run_ends[0] | run_ends[1]
    other_end = jnp.where(run_ends[0], tm + RUN - 1, tm - RUN + 1)
    run_below, run_above = tm >= RUN, tm < lax.axis_size("tm") - RUN
    onward = ((run_ends[1] & run_below, tm - RUN), (run_ends[0] & run_above, tm + RUN))

    def target(r):
        return lax.rem(x + lax.div(r, 2), 4) * 2 + lax.rem(half + lax.rem(r, 2), 2)

    def origin(r):
        return lax.rem(x + 4 - lax.div(r, 2), 4) * 2 + lax.rem(half + lax.rem(r, 2), 2)

    def rows_of(s):
        return pl.ds(pl.multiple_of(s * HEAD, HEAD), HEAD)

    def columns_of(s, j):
        return pl.ds(pl.multiple_of((s * HEADS_HERE + j) * HEAD, HEAD), HEAD)

    def head_columns(j):
        return pl.ds(pl.multiple_of(j * HEAD, HEAD), HEAD)

    sources = (video_k, video_v, video_q, video_g)
    landings = (keys, values, queries, grads)
    results = (out_vo, out_vdq, out_vdk, out_vdv)

    def in_copy(j, a, r, sender):
        s = target(r)
        slot = rows_of(me if sender else origin(r))
        index = (j * 4 + a) * 8 + r
        return pltpu.make_async_remote_copy(
            src_ref=sources[a].at[:, columns_of(s, j)],
            dst_ref=landings[a].at[j, slot, :],
            send_sem=in_send.at[index],
            recv_sem=in_recv.at[index],
            device_id=(tm, s),
            device_id_type=MESH,
        )

    def pool_copy(r):
        s = target(r)
        return pltpu.make_async_remote_copy(
            src_ref=pool_stage.at[s],
            dst_ref=pool_land.at[me],
            send_sem=pool_send.at[r],
            recv_sem=pool_recv.at[r],
            device_id=(tm, s),
            device_id_type=MESH,
        )

    def rows_local(a):
        return pltpu.make_async_copy(sources[a], (rows_k, rows_v)[a], local_rows.at[a])

    def in_local(j, a):
        return pltpu.make_async_copy(
            sources[a].at[:, columns_of(me, j)],
            landings[a].at[j, rows_of(me), :],
            local_in.at[j * 4 + a],
        )

    def out_copy(j, a, r, sender):
        s = target(r)
        slot = columns_of(me if sender else origin(r), j)
        index = (j * 4 + a) * 8 + r
        return pltpu.make_async_remote_copy(
            src_ref=video_out.at[a, j, rows_of(s), :],
            dst_ref=results[a].at[:, slot],
            send_sem=out_send.at[index],
            recv_sem=out_recv.at[index],
            device_id=(tm, s),
            device_id_type=MESH,
        )

    def out_local(j, a):
        return pltpu.make_async_copy(
            video_out.at[a, j, rows_of(me), :],
            results[a].at[:, columns_of(me, j)],
            local_out.at[j * 4 + a],
        )

    sound_sources = (audio_k, audio_v, audio_q, audio_g)

    def sound_local(j, a):
        landing = (
            keys.at[j, pl.ds(OWN, AUDIO), :],
            values.at[j, pl.ds(OWN, AUDIO), :],
            sound_q.at[j],
            sound_g.at[j],
        )[a]
        return pltpu.make_async_copy(
            sound_sources[a].at[:, head_columns(j)], landing, local_sound.at[j * 4 + a]
        )

    sound_results = (out_ao, out_adq, out_adk, out_adv)

    def sound_out(j, a):
        return pltpu.make_async_copy(
            audio_out.at[a, j],
            sound_results[a].at[:, head_columns(j)],
            local_sound_out.at[j * 4 + a],
        )

    def near_copy(src, dst, index, device):
        return pltpu.make_async_remote_copy(
            src_ref=src,
            dst_ref=dst,
            send_sem=near_send.at[index],
            recv_sem=near_recv.at[index],
            device_id=(device, me),
            device_id_type=MESH,
        )

    def rim_copy(j, a, d):
        return near_copy(
            rim_out.at[d, a, j],
            (keys, values)[a].at[j, pl.ds((AFTER, BEFORE)[d], CHUNK), :],
            (j * 2 + a) * 2 + d,
            sides[d][1],
        )

    def relay_copy(j, a, d):
        return pltpu.make_async_remote_copy(
            src_ref=rim_out.at[d, a, j],
            dst_ref=relay_in.at[j, a],
            send_sem=near_send.at[(j * 2 + a) * 2 + d],
            recv_sem=relay_recv.at[j * 2 + a],
            device_id=(other_end, me),
            device_id_type=MESH,
        )

    def onward_copy(j, a, d):
        return pltpu.make_async_remote_copy(
            src_ref=relay_in.at[j, a],
            dst_ref=(keys, values)[a].at[j, pl.ds((AFTER, BEFORE)[d], CHUNK), :],
            send_sem=onward_send.at[j * 2 + a],
            recv_sem=near_recv.at[(j * 2 + a) * 2 + d],
            device_id=(onward[d][1], me),
            device_id_type=MESH,
        )

    def pooled_copy(j, a, d):
        listed = (keys, values)[a]
        return near_copy(
            listed.at[j, pl.ds(SHARED + POOLED, POOLED), :],
            listed.at[j, pl.ds(SHARED + (2 * POOLED, 0)[d], POOLED), :],
            8 + (j * 2 + a) * 2 + d,
            sides[d][1],
        )

    def pool_grad_copy(j, d):
        return near_copy(
            pool_grad_out.at[d, j], pool_grad_in.at[d, j], 16 + j * 2 + d, sides[d][1]
        )

    def rim_grad_copy(j, d, i):
        a, part = i // 4, pl.ds(i % 4 * POOLED, POOLED)
        return near_copy(
            rim_grad_out.at[d, j, a, part, :],
            rim_grad_in.at[d, j, a, part, :],
            20 + (j * 2 + d) * 8 + i,
            sides[d][1],
        )

    def on_sides(act):
        for d in range(2):

            @pl.when(sides[d][0])
            def _():
                act(d)

    def from_sides(act):
        for d in range(2):

            @pl.when(sides[1 - d][0])
            def _():
                act(d)

    barrier = pltpu.get_barrier_semaphore()

    def greet(r, carry):
        pl.semaphore_signal(barrier, inc=1, device_id=(tm, target(r)), device_id_type=MESH)
        return carry

    lax.fori_loop(1, 8, greet, 0)
    on_sides(
        lambda d: pl.semaphore_signal(
            barrier, inc=1, device_id=(sides[d][1], me), device_id_type=MESH
        )
    )
    for there, device in (
        (at_end, other_end),
        (at_end & run_below, tm - RUN),
        (at_end & run_above, tm + RUN),
    ):

        @pl.when(there)
        def _(device=device):
            pl.semaphore_signal(barrier, inc=1, device_id=(device, me), device_id_type=MESH)

    for a in range(2):
        rows_local(a).start()
    for j in range(HEADS_HERE):
        for a in range(4):
            sound_local(j, a).start()
    for j in range(HEADS_HERE):
        for a in range(4):
            in_local(j, a).start()

    for j in range(HEADS_HERE):
        for a in range(2):
            sound_local(j, a).wait()

    def stage_rims(d):
        weight = blocks[1 - d, sides[d][1]].astype(F32)
        for j in range(HEADS_HERE):
            for a in range(2):
                listed = (keys, values)[a]
                first = listed[j, OWN : OWN + CHUNK, :].astype(F32)
                second = listed[j, OWN + CHUNK : BEFORE, :].astype(F32)
                rim_out[d, a, j] = (first * (1.0 - weight) + second * weight).astype(BF16)

    on_sides(stage_rims)

    def fill_rims(d):
        spare = jnp.zeros((HEADS_HERE, CHUNK, HEAD), BF16)
        gone = jnp.zeros((HEADS_HERE, POOLED, HEAD), BF16)
        rim_at, pool_at = (AFTER, BEFORE)[d], SHARED + (2 * POOLED, 0)[d]
        for listed in (keys, values):
            listed[:, rim_at : rim_at + CHUNK, :] = spare
            listed[:, pool_at : pool_at + POOLED, :] = gone
        rim_grad_in[d] = jnp.zeros((HEADS_HERE, 2, CHUNK, HEAD), BF16)
        pool_grad_in[d] = jnp.zeros((HEADS_HERE, 2, POOLED, HEAD), BF16)

    for d in range(2):

        @pl.when(jnp.logical_not(sides[1 - d][0]))
        def _():
            fill_rims(d)

    for listed in (keys, values):
        listed[:, SHARED + 3 * POOLED :, :] = jnp.zeros((HEADS_HERE, POOLED, HEAD), BF16)
    member = lax.broadcasted_iota(jnp.int32, (POOL, HEAD), 0)
    group = lax.shift_right_logical(lax.broadcasted_iota(jnp.int32, (POOL, HEAD), 1), 4)
    upper = jnp.where(member == group, 1.0, 0.0).astype(BF16)
    lower = jnp.where(member == group + 8, 1.0, 0.0).astype(BF16)
    for a in range(2):
        rows_local(a).wait()
    for s in range(8):
        for j in range(HEADS_HERE):
            part = slice((s * HEADS_HERE + j) * HEAD, (s * HEADS_HERE + j + 1) * HEAD)
            both = dot(upper, rows_k[:, part]) + dot(lower, rows_v[:, part])
            pool_stage[s, j] = (both * (POOL**-0.5)).astype(BF16)

    one = jnp.int32(1)
    greeted = 7 + jnp.where(has_prev, one, 0) + jnp.where(has_next, one, 0)
    ends = one + jnp.where(run_below, one, 0) + jnp.where(run_above, one, 0)
    pl.semaphore_wait(barrier, greeted + jnp.where(at_end, ends, 0))

    def to_peers(act):
        lax.fori_loop(1, 8, lambda r, c: (act(r), c)[1], 0)

    def send_in(j, a):
        to_peers(lambda r: in_copy(j, a, r, True).start())

    def sent_in(j, a):
        to_peers(lambda r: in_copy(j, a, r, True).wait_send())

    def came_in(j, a):
        in_local(j, a).wait()
        to_peers(lambda r: in_copy(j, a, r, False).wait_recv())

    def send_out(j, a):
        out_local(j, a).start()
        to_peers(lambda r: out_copy(j, a, r, True).start())

    def send_rims(j):
        def start(a, d):
            @pl.when(run_ends[d])
            def _():
                relay_copy(j, a, d).start()

            @pl.when(jnp.logical_not(run_ends[d]))
            def _():
                rim_copy(j, a, d).start()

        for a in range(2):
            on_sides(lambda d, a=a: start(a, d))

    def pass_on(j):
        for d in range(2):

            @pl.when(onward[d][0])
            def _(d=d):
                for a in range(2):
                    relay_copy(j, a, d).wait_recv()
                    onward_copy(j, a, d).start()

    send_rims(0)
    send_rims(1)
    to_peers(lambda r: pool_copy(r).start())
    send_in(0, 0)
    pass_on(0)
    send_in(0, 1)
    pass_on(1)
    pool_land[me] = pool_stage[me]
    to_peers(lambda r: pool_copy(r).wait_recv())
    for j in range(HEADS_HERE):
        landed = [pool_land[s, j].astype(F32) for s in range(8)]
        for a, listed in enumerate((keys, values)):
            pooled = jnp.concatenate([t[a * 8 : a * 8 + 8] for t in landed], axis=0)
            listed[j, SHARED + POOLED : SHARED + 2 * POOLED, :] = pooled.astype(BF16)
            on_sides(lambda d, j=j, a=a: pooled_copy(j, a, d).start())
    send_in(0, 2)
    send_in(0, 3)
    key_sum[...] = jnp.zeros_like(key_sum)
    value_sum[...] = jnp.zeros_like(value_sum)

    live = (rows[0, tm], rows[1, tm])
    place = lax.broadcasted_iota(jnp.int32, (CHUNK, CHUNK), 0)
    first_pooled = jnp.where(has_prev, 0, POOLED)
    last_pooled = jnp.where(has_next, 3 * POOLED, 2 * POOLED)
    video_chunks = tuple(range(8))
    audio_chunks = (4, 5, 8)

    def mask(c, s):
        if c == 6:
            return jnp.where(place < live[0], s, -jnp.inf)
        if c == 7:
            return jnp.where(place < live[1], s, -jnp.inf)
        if c == 8:
            return jnp.where((place >= first_pooled) & (place < last_pooled), s, -jnp.inf)
        return s

    def span(c):
        return slice(c * CHUNK, (c + 1) * CHUNK)

    def attend(j, chunks, q, g):
        top = None
        for i, c in enumerate(chunks):
            s = mask(c, dot(keys[j, span(c), :], q, ((1,), (1,))))
            scores[span(i), :] = s
            peak = jnp.max(s, axis=0, keepdims=True)
            top = peak if top is None else jnp.maximum(top, peak)
        total = jnp.zeros((1, CHUNK), F32)
        for i, c in enumerate(chunks):
            e = jnp.exp2((scores[span(i), :] - top) * (FACTOR * LOG2E))
            scores[span(i), :] = e
            total = total + jnp.sum(e, axis=0, keepdims=True)
        inverse = 1.0 / total
        output = jnp.zeros((HEAD, CHUNK), F32)
        for i, c in enumerate(chunks):
            p = (scores[span(i), :] * inverse).astype(BF16)
            shares[span(i), :] = p
            output = output + dot(values_t[j, :, span(c)], p)
            value_sum[j, span(c), :] += dot(p, g)
        correction = jnp.sum(g.astype(F32).T * output, axis=0, keepdims=True)
        query_grad = jnp.zeros((HEAD, CHUNK), F32)
        for i, c in enumerate(chunks):
            dp = dot(values[j, span(c), :], g, ((1,), (1,)))
            ds = (shares[span(i), :].astype(F32) * (dp - correction) * FACTOR).astype(BF16)
            query_grad = query_grad + dot(keys_t[j, :, span(c)], ds)
            key_sum[j, span(c), :] += dot(ds, q)
        return output.T.astype(BF16), query_grad.T.astype(BF16)

    def finish(j):
        from_sides(lambda d: pool_grad_copy(j, d).wait_recv())
        for a, summed in enumerate((key_sum, value_sum)):
            pooled = summed[j, SHARED + POOLED : SHARED + 2 * POOLED, :]
            for d in range(2):
                pooled = pooled + pool_grad_in[d, j, a].astype(F32)
            pooled = pooled * (POOL**-0.5)
            spread = jnp.broadcast_to(pooled[:, None, :], (POOLED, POOL, HEAD))
            whole = summed[j, :VIDEO, :] + spread.reshape(VIDEO, HEAD)
            video_out[2 + a, j] = whole.astype(BF16)
            send_out(j, 2 + a)

    def turn(j, c):
        keys_t[j, :, span(c)] = keys[j, span(c), :].astype(F32).T.astype(BF16)
        values_t[j, :, span(c)] = values[j, span(c), :].astype(F32).T.astype(BF16)

    def sound(j, carry):
        turn(j, 4)
        turn(j, 5)
        for a in (2, 3):
            sound_local(j, a).wait()
        for a in range(2):
            from_sides(lambda d, a=a: pooled_copy(j, a, d).wait_recv())
        turn(j, 8)

        def step(i, c):
            part = pl.ds(pl.multiple_of(i * CHUNK, CHUNK), CHUNK)
            o, dq = attend(j, audio_chunks, sound_q[j, part, :], sound_g[j, part, :])
            audio_out[0, j, part, :] = o
            audio_out[1, j, part, :] = dq
            return c

        lax.fori_loop(0, AUDIO // CHUNK, step, 0)
        for d in range(2):
            at = SHARED + (0, 2 * POOLED)[d]
            pool_grad_out[d, j, 0] = key_sum[j, at : at + POOLED, :].astype(BF16)
            pool_grad_out[d, j, 1] = value_sum[j, at : at + POOLED, :].astype(BF16)
        on_sides(lambda d: pool_grad_copy(j, d).start())
        sound_out(j, 0).start()
        sound_out(j, 1).start()

        @pl.when(j == 0)
        def _():
            send_in(1, 0)
            send_in(1, 1)

        return carry

    lax.fori_loop(0, HEADS_HERE, sound, 0)
    send_in(1, 2)
    send_in(1, 3)

    def video(j, carry):
        for a in range(2):
            from_sides(lambda d, a=a: rim_copy(j, a, d).wait_recv())
            came_in(j, a)
        for c in (0, 1, 2, 3, 6, 7):
            turn(j, c)
        came_in(j, 2)
        came_in(j, 3)

        def step(k, c):
            i = lax.rem(x + k, 4)
            part = pl.ds(pl.multiple_of(i * CHUNK, CHUNK), CHUNK)
            o, dq = attend(j, video_chunks, queries[j, part, :], grads[j, part, :])
            video_out[0, j, part, :] = o
            video_out[1, j, part, :] = dq
            for a in range(2):
                out_copy(j, a, 2 * k + 1, True).start()

                @pl.when(k == 0)
                def _(a=a):
                    out_local(j, a).start()

                @pl.when(k > 0)
                def _(a=a):
                    out_copy(j, a, 2 * k, True).start()

            return c

        lax.fori_loop(0, 4, step, 0)
        for d in range(2):
            at = (BEFORE, AFTER)[d]
            rim_grad_out[d, j, 0] = key_sum[j, at : at + CHUNK, :].astype(BF16)
            rim_grad_out[d, j, 1] = value_sum[j, at : at + CHUNK, :].astype(BF16)
        for i in range(8):
            on_sides(lambda d, i=i: rim_grad_copy(j, d, i).start())
        finish(j)
        return carry

    lax.fori_loop(0, HEADS_HERE, video, 0)

    prev_weight = blocks[1, jnp.maximum(tm - 1, 0)].astype(F32)
    next_weight = blocks[0, jnp.minimum(tm + 1, lax.axis_size("tm") - 1)].astype(F32)
    weights = (next_weight, prev_weight)
    for j in range(HEADS_HERE):
        for i in range(8):
            from_sides(lambda d, j=j, i=i: rim_grad_copy(j, d, i).wait_recv())
        for a in range(2):
            for b in range(2):
                part = slice(b * CHUNK, (b + 1) * CHUNK)
                whole = (key_sum, value_sum)[a][j, OWN + b * CHUNK : OWN + (b + 1) * CHUNK, :]
                for d in range(2):
                    weight = weights[d] if b else 1.0 - weights[d]
                    whole = whole + rim_grad_in[d, j, a].astype(F32) * weight
                audio_out[2 + a, j, part, :] = whole.astype(BF16)
            sound_out(j, 2 + a).start()

    for j in range(HEADS_HERE):
        for a in range(4):
            sound_out(j, a).wait()
            out_local(j, a).wait()
            to_peers(lambda r, j=j, a=a: out_copy(j, a, r, True).wait_send())
            to_peers(lambda r, j=j, a=a: out_copy(j, a, r, False).wait_recv())
        for a in range(2):
            on_sides(lambda d, j=j, a=a: rim_copy(j, a, d).wait_send())
            on_sides(lambda d, j=j, a=a: pooled_copy(j, a, d).wait_send())
        on_sides(lambda d, j=j: pool_grad_copy(j, d).wait_send())
        for i in range(8):
            on_sides(lambda d, j=j, i=i: rim_grad_copy(j, d, i).wait_send())
    for j in range(HEADS_HERE):
        for a in range(4):
            sent_in(j, a)
    to_peers(lambda r: pool_copy(r).wait_send())
    for d in range(2):

        @pl.when(onward[d][0])
        def _(d=d):
            for j in range(HEADS_HERE):
                for a in range(2):
                    onward_copy(j, a, d).wait_send()


def publish(*refs):
    sem = refs[16]
    copies = [pltpu.make_async_copy(refs[i], refs[8 + i], sem.at[i]) for i in range(8)]
    for copy in copies:
        copy.start()
    for copy in copies:
        copy.wait()


def per_device(*args):
    video = jax.ShapeDtypeStruct(args[0].shape, BF16)
    audio = jax.ShapeDtypeStruct(args[4].shape, BF16)
    two = HEADS_HERE
    made = pl.pallas_call(
        kernel,
        out_shape=(pltpu.VMEM(video.shape, BF16),) * 4 + (pltpu.VMEM(audio.shape, BF16),) * 4,
        in_specs=[pl.BlockSpec(memory_space=pltpu.HBM)] * 8
        + [pl.BlockSpec(memory_space=pltpu.SMEM)] * 2,
        out_specs=(pl.BlockSpec(memory_space=pltpu.VMEM),) * 8,
        scratch_shapes=[
            pltpu.VMEM((two, LISTED, HEAD), BF16),
            pltpu.VMEM((two, LISTED, HEAD), BF16),
            pltpu.VMEM((two, VIDEO, HEAD), BF16),
            pltpu.VMEM((two, VIDEO, HEAD), BF16),
            pltpu.VMEM((two, AUDIO, HEAD), BF16),
            pltpu.VMEM((two, AUDIO, HEAD), BF16),
            pltpu.VMEM((two, HEAD, LISTED), BF16),
            pltpu.VMEM((two, HEAD, LISTED), BF16),
            pltpu.VMEM((two, LISTED, HEAD), F32),
            pltpu.VMEM((two, LISTED, HEAD), F32),
            pltpu.VMEM((SHARED, CHUNK), F32),
            pltpu.VMEM((SHARED, CHUNK), BF16),
            pltpu.VMEM((HEAD, 8 * two * HEAD), BF16),
            pltpu.VMEM((HEAD, 8 * two * HEAD), BF16),
            pltpu.VMEM((8, two, POOL, HEAD), BF16),
            pltpu.VMEM((8, two, POOL, HEAD), BF16),
            pltpu.VMEM((4, two, VIDEO, HEAD), BF16),
            pltpu.VMEM((4, two, AUDIO, HEAD), BF16),
            pltpu.VMEM((2, 2, two, CHUNK, HEAD), BF16),
            pltpu.VMEM((two, 2, CHUNK, HEAD), BF16),
            pltpu.VMEM((2, two, 2, CHUNK, HEAD), BF16),
            pltpu.VMEM((2, two, 2, CHUNK, HEAD), BF16),
            pltpu.VMEM((2, two, 2, POOLED, HEAD), BF16),
            pltpu.VMEM((2, two, 2, POOLED, HEAD), BF16),
            pltpu.SemaphoreType.DMA((64,)),
            pltpu.SemaphoreType.DMA((64,)),
            pltpu.SemaphoreType.DMA((64,)),
            pltpu.SemaphoreType.DMA((64,)),
            pltpu.SemaphoreType.DMA((52,)),
            pltpu.SemaphoreType.DMA((52,)),
            pltpu.SemaphoreType.DMA((8,)),
            pltpu.SemaphoreType.DMA((8,)),
            pltpu.SemaphoreType.DMA((4,)),
            pltpu.SemaphoreType.DMA((4,)),
            pltpu.SemaphoreType.DMA((2,)),
            pltpu.SemaphoreType.DMA((8,)),
            pltpu.SemaphoreType.DMA((8,)),
            pltpu.SemaphoreType.DMA((8,)),
            pltpu.SemaphoreType.DMA((8,)),
        ],
        compiler_params=pltpu.CompilerParams(
            collective_id=0, has_side_effects=True, vmem_limit_bytes=60 * 1024 * 1024
        ),
        name="joint_attention",
    )(*args[:8], args[8].T, args[9].T)
    return pl.pallas_call(
        publish,
        out_shape=(video,) * 4 + (audio,) * 4,
        in_specs=[pl.BlockSpec(memory_space=pl.ANY)] * 8,
        out_specs=(pl.BlockSpec(memory_space=pltpu.HBM),) * 8,
        scratch_shapes=[pltpu.SemaphoreType.DMA((8,))],
        compiler_params=pltpu.CompilerParams(vmem_limit_bytes=1024 * 1024),
        name="publish",
    )(*made)


def solution(mesh):
    tokens, sound = P(("tm", "space"), None), P("tm", "space")
    return jax.shard_map(
        per_device,
        mesh=mesh,
        in_specs=(tokens,) * 4 + (sound,) * 4 + (P(), P()),
        out_specs=(tokens,) * 4 + (sound,) * 4,
        check_vma=False,
    )
```
